32 devices in a mesh: row: 8 (over z, y), col: 4 (over x, core).
Axes of the slice: x: 2, y: 2, z: 4, core: 2. Of those that a mesh axis runs over, the one named last changes fastest.
Arguments:
- embeddings: bfloat16 [512, 256], P(('row', 'col')), may hold values from -6 to 6
- labels: bfloat16 [512, 1024], P(('row', 'col')), may hold values from -6 to 6
- tile_mask: int32 [2, 2], replicated, may hold values 0 or 1
Outputs:
- spread_labels: bfloat16 [512, 1024], P(('row', 'col'))
The draws below stay inside these ranges and needn't reach their ends.
Inputs may be any that keep to these rules, and one draw needn't show every extreme that they name: Only the entries tile_mask[i, j] with i < j are read; the tile of blocks i and j (and of j and i) is kept where it is 1.
All inputs are finite; a program needn't handle non-finite values.
Results may differ from the reference program's by a relative error of at most 0.015.
Values may be sent and summed in bfloat16 or wider, within the bound.
No kernel may reach another device: no remote copies, remote signals or barrier semaphores. Data moves between devices by JAX's collectives and lax.ppermute only.
A program may use at most 64 MiB of HBM per device.

```python
import math
import jax
import jax.numpy as jnp
from jax import lax

E = 256
C = 1024
BLOCK = 256
ITERS = 2
IMAGES = 512
BLOCKS = 2


def place_ends(array, own_key, smallest, high):
    longest = array.shape.index(max(array.shape))
    spots = []
    for shift in (0, 1):
        where = [jax.random.randint(jax.random.fold_in(own_key, axis), (), 0, length) for axis, length in enumerate(array.shape)]
        where[longest] = (where[longest] + shift) % array.shape[longest]
        spots.append(tuple(where))
    return array.at[spots[0]].set(smallest).at[spots[1]].set(high)


def level_of(rng, dims, shards, low, high):
    loudness = 1.0
    for position, shards_of in shards:
        heights = jax.random.uniform(jax.random.fold_in(jax.random.fold_in(rng, 6), position), (shards_of,), jnp.float32, low / len(shards), high / len(shards))
        loudness = loudness * jnp.repeat(jnp.exp(heights), dims[position] // shards_of).reshape((-1,) + (1,) * (len(dims) - 1 - position))
    return loudness


def noise(rng, dims, scale, limit, split=(), held_as=jnp.bfloat16):
    values = jax.random.normal(rng, dims, jnp.float32) * scale
    if len(split) > 0:
        values = level_of(rng, dims, split, -0.22, 0.18) * values
    return jnp.clip(values, min=-limit, max=limit).astype(held_as)


def setup_inputs(seed: int = 0) -> dict:
    streams_of = jax.random.split(jax.random.key(seed), 4)
    return {
        "embeddings": noise(streams_of[0], (IMAGES, E), 1.0, 6.0, ((0, 32),)),
        "labels": noise(streams_of[1], (IMAGES, C), 1.0, 6.0, ((0, 32),)),
        "tile_mask": place_ends((jax.random.randint(streams_of[2], (BLOCKS, BLOCKS), 0, 4) < 3).astype(jnp.int32), jax.random.fold_in(streams_of[2], 1), 0, 1),
    }


MIXING = 0.9
SHARPNESS = 3.0
EPSILON = 1e-06

def unit_rows(embeddings):
    values = embeddings.astype(jnp.float32)
    return (values * lax.rsqrt(lax.optimization_barrier(jnp.sum(values * values, axis=1, keepdims=True)) + EPSILON)).astype(jnp.bfloat16)

def symmetric_keep(tile_mask):
    blocks = tile_mask.shape[0]
    block_row = lax.broadcasted_iota(jnp.int32, (blocks, blocks), 0)
    block_col = lax.broadcasted_iota(jnp.int32, (blocks, blocks), 1)
    mirrored = jnp.where(block_row < block_col, tile_mask, tile_mask.T)
    return jnp.where(block_row == block_col, 1, mirrored)

def reference(embeddings, labels, tile_mask):
    unit_vecs = unit_rows(embeddings)
    kept_sym = symmetric_keep(tile_mask).astype(jnp.float32)
    sharpness = SHARPNESS * math.sqrt(E)
    all_ids = jnp.arange(IMAGES, dtype=jnp.int32)
    block_list = jnp.arange(BLOCKS, dtype=jnp.int32)

    def kernel_block(block_index):
        offset_rows = (block_index * BLOCK).astype(jnp.int32)
        block_vecs = lax.dynamic_slice_in_dim(unit_vecs, offset_rows, BLOCK, 0)
        cosine = jnp.dot(block_vecs, unit_vecs.T, preferred_element_type=jnp.float32)
        kept_row = jnp.repeat(kept_sym[block_index], BLOCK)
        own_ids = offset_rows + jnp.arange(BLOCK, dtype=jnp.int32)
        distinct = own_ids[:, None] != all_ids[None, :]
        return jnp.where(distinct, jnp.exp(sharpness * cosine) * kept_row[None, :], jnp.zeros_like(cosine)).astype(jnp.bfloat16)
    degree = lax.map(lambda index: lax.optimization_barrier(jnp.sum(kernel_block(index), axis=1, dtype=jnp.float32)), block_list).reshape(IMAGES)
    inv_root = lax.rsqrt(degree)
    seed_scores = labels.astype(jnp.float32)
    current = seed_scores
    for iteration in range(ITERS):
        scaled = (inv_root[:, None] * current).astype(jnp.bfloat16)
        spread = lax.map(lambda index: jnp.dot(kernel_block(index), scaled, preferred_element_type=jnp.float32), block_list).reshape(IMAGES, C)
        current = MIXING * inv_root[:, None] * spread + (1.0 - MIXING) * seed_scores
    return current.astype(jnp.bfloat16)
```

```python
import functools
import math

import jax
import jax.numpy as jnp
from jax import lax
from jax.experimental import pallas as pl
from jax.experimental.pallas import tpu as pltpu
from jax.sharding import PartitionSpec as P

BLOCK = 256
ITERS = 2


MIXING = 0.9
SHARPNESS = 3.0
EPSILON = 1e-06


def unit_rows(embeddings):
    values = embeddings.astype(jnp.float32)
    return (values * lax.rsqrt(jnp.sum(values * values, axis=1, keepdims=True) + EPSILON)).astype(
        jnp.bfloat16
    )


def symmetric_keep(tile_mask):
    blocks = tile_mask.shape[0]
    block_row = lax.broadcasted_iota(jnp.int32, (blocks, blocks), 0)
    block_col = lax.broadcasted_iota(jnp.int32, (blocks, blocks), 1)
    mirrored = jnp.where(block_row < block_col, tile_mask, tile_mask.T)
    return (jnp.where(block_row == block_col, 1, mirrored), block_row, block_col)


def rotate_rows(values, start):
    total = values.shape[0]
    doubled = jnp.concatenate([values, values], axis=0)
    return lax.dynamic_slice_in_dim(doubled, start, total, 0)


def one_term(operands):
    row_kernel, part_labels = operands
    return jnp.dot(row_kernel, part_labels, preferred_element_type=jnp.float32)


def no_term(operands):
    row_kernel, part_labels = operands
    return jnp.zeros((row_kernel.shape[0], part_labels.shape[1]), jnp.float32)


def shards(embeddings, labels, tile_mask):
    row_count = lax.axis_size("row")
    col_count = lax.axis_size("col")
    row_index = lax.axis_index("row")
    col_index = lax.axis_index("col")
    piece_rows = embeddings.shape[0]
    emb_width = embeddings.shape[1]
    channels = labels.shape[1]
    blocks = tile_mask.shape[0]
    sharpness = SHARPNESS * math.sqrt(emb_width)
    unit_vecs = unit_rows(embeddings)
    row_units = lax.all_gather(unit_vecs, "col", axis=0, tiled=True)
    col_gathered = lax.all_gather(unit_vecs, "row", axis=0, tiled=True)
    row_total = row_units.shape[0]
    col_total = col_gathered.shape[0]
    shift = row_index * piece_rows
    col_units = rotate_rows(col_gathered, shift)
    unit_count = math.gcd(8, row_count)
    unit_width = col_total // unit_count
    kept_sym, block_row, block_col = symmetric_keep(tile_mask)
    global_rows = row_index * row_total + jnp.arange(row_total, dtype=jnp.int32)
    row_blocks = global_rows // BLOCK
    block_ids = jnp.arange(blocks, dtype=jnp.int32)
    row_onehot = (row_blocks[:, None] == block_ids[None, :]).astype(jnp.bfloat16)
    row_table = jnp.dot(
        row_onehot, kept_sym.astype(jnp.bfloat16), preferred_element_type=jnp.float32
    ).astype(jnp.bfloat16)
    local_cols = (jnp.arange(col_total, dtype=jnp.int32) + shift) % col_total
    global_cols = (
        local_cols // piece_rows * col_count + col_index
    ) * piece_rows + local_cols % piece_rows
    col_blocks = global_cols // BLOCK
    kernels_row = []
    active_flags = []
    row_degree = jnp.zeros((row_total,), jnp.float32)
    for column_unit in range(unit_count):
        offset_cols = column_unit * unit_width
        part_units = col_units[offset_cols : offset_cols + unit_width]
        part_blocks = col_blocks[offset_cols : offset_cols + unit_width]
        part_cols = global_cols[offset_cols : offset_cols + unit_width]
        col_onehot = (part_blocks[:, None] == block_ids[None, :]).astype(jnp.bfloat16)
        kept_mask = lax.dot_general(
            row_table, col_onehot, (((1,), (1,)), ((), ())), preferred_element_type=jnp.float32
        )
        cosine = lax.dot_general(
            row_units, part_units, (((1,), (1,)), ((), ())), preferred_element_type=jnp.float32
        )
        distinct = global_rows[:, None] != part_cols[None, :]
        weights = jnp.where(
            distinct, jnp.exp(sharpness * cosine) * kept_mask, jnp.zeros_like(cosine)
        ).astype(jnp.bfloat16)
        active_flags.append(jnp.sum(kept_mask) > 0.0)
        kernels_row.append(weights)
        row_degree = row_degree + jnp.sum(weights, axis=1, dtype=jnp.float32)
    degree = lax.psum_scatter(row_degree, "col", scatter_dimension=0, tiled=True)
    inv_root = lax.rsqrt(degree)
    seed_scores = labels.astype(jnp.float32)
    current = seed_scores
    for iteration in range(ITERS):
        scaled = (inv_root[:, None] * current).astype(jnp.bfloat16)
        col_labels = rotate_rows(lax.all_gather(scaled, "row", axis=0, tiled=True), shift)
        row_sum = jnp.zeros((row_total, channels), jnp.float32)
        for column_unit in range(unit_count):
            offset_cols = column_unit * unit_width
            part_labels = col_labels[offset_cols : offset_cols + unit_width]
            row_sum = row_sum + lax.cond(
                active_flags[column_unit],
                one_term,
                no_term,
                (kernels_row[column_unit], part_labels),
            )
        sent_rows = row_sum.astype(jnp.bfloat16).reshape(col_count, piece_rows, channels)
        arrived = lax.all_to_all(sent_rows, "col", split_axis=0, concat_axis=0, tiled=True)
        spread = jnp.sum(arrived, axis=0, dtype=jnp.float32)
        current = MIXING * inv_root[:, None] * spread + (1.0 - MIXING) * seed_scores
    return current.astype(jnp.bfloat16)


AXES = ("row", "col")
LANES = 128
WHOLE_KERNEL_BYTES = 4 * 1024 * 1024


def pack_body(emb_ref, lab_ref, sent_ref):
    peers, _, width = sent_ref.shape
    emb_width = emb_ref.shape[1]
    lanes = width - emb_width
    near = lab_ref.shape[1] // lanes
    unit_vecs = unit_rows(emb_ref[...])
    for peer in range(peers):
        first = peer % near * lanes
        sent_ref[peer, :, :emb_width] = unit_vecs
        sent_ref[peer, :, emb_width:] = lab_ref[:, first : first + lanes]


def spread_body(emb_width, mask_ref, start_ref, all_ref, out_ref, kernel_ref):
    images = all_ref.shape[0]
    lanes = out_ref.shape[1]
    blocks = images // BLOCK
    sharpness = SHARPNESS * math.sqrt(emb_width)
    for i in range(blocks):
        rows = slice(i * BLOCK, (i + 1) * BLOCK)
        for j in range(blocks):
            cols = slice(j * BLOCK, (j + 1) * BLOCK)
            cosine = lax.dot_general(
                all_ref[rows, :emb_width],
                all_ref[cols, :emb_width],
                (((1,), (1,)), ((), ())),
                preferred_element_type=jnp.float32,
            )
            weights = jnp.exp(sharpness * cosine)
            if i == j:
                row_ids = lax.broadcasted_iota(jnp.int32, weights.shape, 0)
                col_ids = lax.broadcasted_iota(jnp.int32, weights.shape, 1)
                weights = jnp.where(row_ids == col_ids, 0.0, weights)
            else:
                weights = weights * mask_ref[min(i, j), max(i, j)].astype(jnp.float32)
            kernel_ref[rows, cols] = weights.astype(jnp.bfloat16)
    labels = all_ref[:, emb_width:].astype(jnp.float32)
    weights = kernel_ref[...]
    degree = jnp.dot(
        weights, jnp.ones((images, lanes), jnp.bfloat16), preferred_element_type=jnp.float32
    )
    inv_root = lax.rsqrt(degree)
    current = labels
    for iteration in range(ITERS - 1):
        scaled = (inv_root * current).astype(jnp.bfloat16)
        spread = jnp.dot(weights, scaled, preferred_element_type=jnp.float32)
        current = MIXING * inv_root * spread + (1.0 - MIXING) * labels
    scaled = (inv_root * current).astype(jnp.bfloat16)
    own_rows = pl.ds(pl.multiple_of(start_ref[0], 16), out_ref.shape[0])
    own_weights = kernel_ref[own_rows, :]
    own_degree = jnp.dot(
        own_weights, jnp.ones((images, lanes), jnp.bfloat16), preferred_element_type=jnp.float32
    )
    spread = jnp.dot(own_weights, scaled, preferred_element_type=jnp.float32)
    own_labels = all_ref[own_rows, emb_width:].astype(jnp.float32)
    out_ref[...] = (
        MIXING * lax.rsqrt(own_degree) * spread + (1.0 - MIXING) * own_labels
    ).astype(jnp.bfloat16)


def whole_shards(embeddings, labels, tile_mask):
    piece_rows, emb_width = embeddings.shape
    channels = labels.shape[1]
    lanes = LANES
    near = channels // lanes
    peers = lax.axis_size(AXES)
    groups = [list(range(first, first + near)) for first in range(0, peers, near)]
    images = peers * piece_rows
    width = emb_width + lanes
    vmem = pl.BlockSpec(memory_space=pltpu.VMEM)
    smem = pl.BlockSpec(memory_space=pltpu.SMEM)
    sent = pl.pallas_call(
        pack_body,
        out_shape=jax.ShapeDtypeStruct((peers, piece_rows, width), jnp.bfloat16),
        in_specs=[vmem, vmem],
        out_specs=vmem,
    )(embeddings, labels)
    arrived = lax.all_to_all(sent, AXES, split_axis=0, concat_axis=0, tiled=True)
    group_rows = near * piece_rows
    start = (lax.axis_index(AXES) // near * group_rows).astype(jnp.int32).reshape(1)
    group_out = pl.pallas_call(
        functools.partial(spread_body, emb_width),
        out_shape=jax.ShapeDtypeStruct((group_rows, lanes), jnp.bfloat16),
        in_specs=[smem, smem, vmem],
        out_specs=vmem,
        scratch_shapes=[pltpu.VMEM((images, images), jnp.bfloat16)],
        compiler_params=pltpu.CompilerParams(vmem_limit_bytes=32 * 1024 * 1024),
    )(tile_mask, start, arrived.reshape(images, width))
    pieces = lax.all_to_all(
        group_out.reshape(near, piece_rows, lanes),
        AXES,
        split_axis=0,
        concat_axis=0,
        axis_index_groups=groups,
        tiled=True,
    )
    return pieces.transpose(1, 0, 2).reshape(piece_rows, channels)


def solution(mesh):
    placed = (P(AXES, None), P(AXES, None), P())
    devices = mesh.devices.size

    def spread_labels(embeddings, labels, tile_mask):
        images = embeddings.shape[0]
        channels = labels.shape[1]
        whole = (
            images * images * 2 <= WHOLE_KERNEL_BYTES
            and images % (devices * 16) == 0
            and images % BLOCK == 0
            and channels % LANES == 0
            and devices % (channels // LANES) == 0
        )
        return jax.shard_map(
            whole_shards if whole else shards,
            mesh=mesh,
            in_specs=placed,
            out_specs=P(AXES, None),
            check_vma=False,
        )(embeddings, labels, tile_mask)

    return spread_labels
```

```python
import functools
import math

import jax
import jax.numpy as jnp
from jax import lax
from jax.experimental import pallas as pl
from jax.experimental.pallas import tpu as pltpu
from jax.sharding import PartitionSpec as P

BLOCK = 256
ITERS = 2


MIXING = 0.9
SHARPNESS = 3.0
EPSILON = 1e-06


def unit_rows(embeddings):
    values = embeddings.astype(jnp.float32)
    return (values * lax.rsqrt(jnp.sum(values * values, axis=1, keepdims=True) + EPSILON)).astype(
        jnp.bfloat16
    )


def symmetric_keep(tile_mask):
    blocks = tile_mask.shape[0]
    block_row = lax.broadcasted_iota(jnp.int32, (blocks, blocks), 0)
    block_col = lax.broadcasted_iota(jnp.int32, (blocks, blocks), 1)
    mirrored = jnp.where(block_row < block_col, tile_mask, tile_mask.T)
    return (jnp.where(block_row == block_col, 1, mirrored), block_row, block_col)


def rotate_rows(values, start):
    total = values.shape[0]
    doubled = jnp.concatenate([values, values], axis=0)
    return lax.dynamic_slice_in_dim(doubled, start, total, 0)


def one_term(operands):
    row_kernel, part_labels = operands
    return jnp.dot(row_kernel, part_labels, preferred_element_type=jnp.float32)


def no_term(operands):
    row_kernel, part_labels = operands
    return jnp.zeros((row_kernel.shape[0], part_labels.shape[1]), jnp.float32)


def shards(embeddings, labels, tile_mask):
    row_count = lax.axis_size("row")
    col_count = lax.axis_size("col")
    row_index = lax.axis_index("row")
    col_index = lax.axis_index("col")
    piece_rows = embeddings.shape[0]
    emb_width = embeddings.shape[1]
    channels = labels.shape[1]
    blocks = tile_mask.shape[0]
    sharpness = SHARPNESS * math.sqrt(emb_width)
    unit_vecs = unit_rows(embeddings)
    row_units = lax.all_gather(unit_vecs, "col", axis=0, tiled=True)
    col_gathered = lax.all_gather(unit_vecs, "row", axis=0, tiled=True)
    row_total = row_units.shape[0]
    col_total = col_gathered.shape[0]
    shift = row_index * piece_rows
    col_units = rotate_rows(col_gathered, shift)
    unit_count = math.gcd(8, row_count)
    unit_width = col_total // unit_count
    kept_sym, block_row, block_col = symmetric_keep(tile_mask)
    global_rows = row_index * row_total + jnp.arange(row_total, dtype=jnp.int32)
    row_blocks = global_rows // BLOCK
    block_ids = jnp.arange(blocks, dtype=jnp.int32)
    row_onehot = (row_blocks[:, None] == block_ids[None, :]).astype(jnp.bfloat16)
    row_table = jnp.dot(
        row_onehot, kept_sym.astype(jnp.bfloat16), preferred_element_type=jnp.float32
    ).astype(jnp.bfloat16)
    local_cols = (jnp.arange(col_total, dtype=jnp.int32) + shift) % col_total
    global_cols = (
        local_cols // piece_rows * col_count + col_index
    ) * piece_rows + local_cols % piece_rows
    col_blocks = global_cols // BLOCK
    kernels_row = []
    active_flags = []
    row_degree = jnp.zeros((row_total,), jnp.float32)
    for column_unit in range(unit_count):
        offset_cols = column_unit * unit_width
        part_units = col_units[offset_cols : offset_cols + unit_width]
        part_blocks = col_blocks[offset_cols : offset_cols + unit_width]
        part_cols = global_cols[offset_cols : offset_cols + unit_width]
        col_onehot = (part_blocks[:, None] == block_ids[None, :]).astype(jnp.bfloat16)
        kept_mask = lax.dot_general(
            row_table, col_onehot, (((1,), (1,)), ((), ())), preferred_element_type=jnp.float32
        )
        cosine = lax.dot_general(
            row_units, part_units, (((1,), (1,)), ((), ())), preferred_element_type=jnp.float32
        )
        distinct = global_rows[:, None] != part_cols[None, :]
        weights = jnp.where(
            distinct, jnp.exp(sharpness * cosine) * kept_mask, jnp.zeros_like(cosine)
        ).astype(jnp.bfloat16)
        active_flags.append(jnp.sum(kept_mask) > 0.0)
        kernels_row.append(weights)
        row_degree = row_degree + jnp.sum(weights, axis=1, dtype=jnp.float32)
    degree = lax.psum_scatter(row_degree, "col", scatter_dimension=0, tiled=True)
    inv_root = lax.rsqrt(degree)
    seed_scores = labels.astype(jnp.float32)
    current = seed_scores
    for iteration in range(ITERS):
        scaled = (inv_root[:, None] * current).astype(jnp.bfloat16)
        col_labels = rotate_rows(lax.all_gather(scaled, "row", axis=0, tiled=True), shift)
        row_sum = jnp.zeros((row_total, channels), jnp.float32)
        for column_unit in range(unit_count):
            offset_cols = column_unit * unit_width
            part_labels = col_labels[offset_cols : offset_cols + unit_width]
            row_sum = row_sum + lax.cond(
                active_flags[column_unit],
                one_term,
                no_term,
                (kernels_row[column_unit], part_labels),
            )
        sent_rows = row_sum.astype(jnp.bfloat16).reshape(col_count, piece_rows, channels)
        arrived = lax.all_to_all(sent_rows, "col", split_axis=0, concat_axis=0, tiled=True)
        spread = jnp.sum(arrived, axis=0, dtype=jnp.float32)
        current = MIXING * inv_root[:, None] * spread + (1.0 - MIXING) * seed_scores
    return current.astype(jnp.bfloat16)


AXES = ("row", "col")
SHARE = 256
WHOLE_KERNEL_BYTES = 4 * 1024 * 1024


def pack_body(emb_hbm, lab_hbm, mask_hbm, sent_ref, kept_ref, emb_ref, lab_ref, sems):
    copies = [
        pltpu.make_async_copy(source, target, sems.at[k])
        for k, (source, target) in enumerate(
            ((emb_hbm, emb_ref), (lab_hbm, lab_ref), (mask_hbm, kept_ref))
        )
    ]
    for copy in copies:
        copy.start()
    peers, _, width = sent_ref.shape
    emb_width = emb_ref.shape[1]
    share = width - emb_width
    team = lab_ref.shape[1] // share
    copies[0].wait()
    unit_vecs = unit_rows(emb_ref[...])
    for peer in range(peers):
        sent_ref[peer, :, :emb_width] = unit_vecs
    copies[1].wait()
    for peer in range(peers):
        first = peer % team * share
        sent_ref[peer, :, emb_width:] = lab_ref[:, first : first + share]
    copies[2].wait()


def spread_body(emb_width, start_ref, kept_ref, mine_ref, theirs_ref, out_ref, kernel_ref):
    half = mine_ref.shape[0]
    images = 2 * half
    share = out_ref.shape[1]
    segment = BLOCK // 2
    blocks = half // segment
    sharpness = SHARPNESS * math.sqrt(emb_width)
    halves = (mine_ref, theirs_ref)
    for s in range(2):
        for t in range(2):
            cosine = lax.dot_general(
                halves[s][:, :emb_width],
                halves[t][:, :emb_width],
                (((1,), (1,)), ((), ())),
                preferred_element_type=jnp.float32,
            )
            weights = jnp.exp(sharpness * cosine)
            for i in range(blocks):
                for j in range(blocks):
                    part = weights[
                        i * segment : (i + 1) * segment, j * segment : (j + 1) * segment
                    ]
                    if i != j:
                        low, high = min(i, j), max(i, j)
                        part = part * kept_ref[low : low + 1, high : high + 1].astype(jnp.float32)
                    elif s == t:
                        row_ids = lax.broadcasted_iota(jnp.int32, part.shape, 0)
                        col_ids = lax.broadcasted_iota(jnp.int32, part.shape, 1)
                        part = jnp.where(row_ids == col_ids, 0.0, part)
                    row = s * half + i * segment
                    col = t * half + j * segment
                    kernel_ref[row : row + segment, col : col + segment] = part.astype(jnp.bfloat16)
    labels = jnp.concatenate([mine_ref[:, emb_width:], theirs_ref[:, emb_width:]], axis=0).astype(
        jnp.float32
    )
    weights = kernel_ref[...]
    ones = jnp.ones((images, share), jnp.bfloat16)
    inv_root = lax.rsqrt(jnp.dot(weights, ones, preferred_element_type=jnp.float32))
    current = labels
    for iteration in range(ITERS - 1):
        scaled = (inv_root * current).astype(jnp.bfloat16)
        spread = jnp.dot(weights, scaled, preferred_element_type=jnp.float32)
        current = MIXING * inv_root * spread + (1.0 - MIXING) * labels
    scaled = (inv_root * current).astype(jnp.bfloat16)
    own_rows = pl.ds(pl.multiple_of(start_ref[0], 16), out_ref.shape[0])
    own_weights = kernel_ref[own_rows, :]
    own_root = lax.rsqrt(jnp.dot(own_weights, ones, preferred_element_type=jnp.float32))
    spread = jnp.dot(own_weights, scaled, preferred_element_type=jnp.float32)
    own_labels = mine_ref[own_rows, emb_width:].astype(jnp.float32)
    out_ref[...] = (MIXING * own_root * spread + (1.0 - MIXING) * own_labels).astype(jnp.bfloat16)


def whole_shards(embeddings, labels, tile_mask):
    piece_rows, emb_width = embeddings.shape
    channels = labels.shape[1]
    team = channels // SHARE
    devices = lax.axis_size(AXES)
    peers = devices // 2
    half = peers * piece_rows
    width = emb_width + SHARE
    same_core = [list(range(core, devices, 2)) for core in range(2)]
    teams = [
        list(range(first + core, first + 2 * team, 2))
        for first in range(0, devices, 2 * team)
        for core in range(2)
    ]
    vmem = pl.BlockSpec(memory_space=pltpu.VMEM)
    hbm = pl.BlockSpec(memory_space=pltpu.HBM)
    smem = pl.BlockSpec(memory_space=pltpu.SMEM)
    sent, kept = pl.pallas_call(
        pack_body,
        out_shape=(
            jax.ShapeDtypeStruct((peers, piece_rows, width), jnp.bfloat16),
            jax.ShapeDtypeStruct(tile_mask.shape, jnp.int32),
        ),
        in_specs=[hbm, hbm, hbm],
        out_specs=(vmem, vmem),
        scratch_shapes=[
            pltpu.VMEM(embeddings.shape, embeddings.dtype),
            pltpu.VMEM(labels.shape, labels.dtype),
            pltpu.SemaphoreType.DMA((3,)),
        ],
        compiler_params=pltpu.CompilerParams(vmem_limit_bytes=8 * 1024 * 1024),
    )(*(pltpu.with_memory_space_constraint(x, pltpu.HBM) for x in (embeddings, labels, tile_mask)))
    mine = lax.all_to_all(
        sent, AXES, split_axis=0, concat_axis=0, axis_index_groups=same_core, tiled=True
    ).reshape(half, width)
    theirs = lax.ppermute(mine, AXES, [(i, i ^ 1) for i in range(devices)])
    team_rows = team * piece_rows
    start = (lax.axis_index(AXES) // (2 * team) * team_rows).astype(jnp.int32).reshape(1)
    team_out = pl.pallas_call(
        functools.partial(spread_body, emb_width),
        out_shape=jax.ShapeDtypeStruct((team_rows, SHARE), jnp.bfloat16),
        in_specs=[smem, vmem, vmem, vmem],
        out_specs=vmem,
        scratch_shapes=[pltpu.VMEM((2 * half, 2 * half), jnp.bfloat16)],
        compiler_params=pltpu.CompilerParams(vmem_limit_bytes=32 * 1024 * 1024),
    )(start, kept, mine, theirs)
    pieces = lax.all_to_all(
        team_out.reshape(team, piece_rows, SHARE),
        AXES,
        split_axis=0,
        concat_axis=0,
        axis_index_groups=teams,
        tiled=True,
    )
    return pieces.transpose(1, 0, 2).reshape(piece_rows, channels)


def solution(mesh):
    placed = (P(AXES, None), P(AXES, None), P())
    devices = mesh.devices.size

    def spread_labels(embeddings, labels, tile_mask):
        images = embeddings.shape[0]
        channels = labels.shape[1]
        whole = (
            images * images * 2 <= WHOLE_KERNEL_BYTES
            and images % (devices * 16) == 0
            and images % BLOCK == 0
            and BLOCK % (images // devices * 2) == 0
            and channels % SHARE == 0
            and devices % (channels // SHARE * 2) == 0
        )
        return jax.shard_map(
            whole_shards if whole else shards,
            mesh=mesh,
            in_specs=placed,
            out_specs=P(AXES, None),
            check_vma=False,
        )(embeddings, labels, tile_mask)

    return spread_labels
```

```python
import functools
import math

import jax
import jax.numpy as jnp
from jax import lax
from jax.experimental import pallas as pl
from jax.experimental.pallas import tpu as pltpu
from jax.sharding import PartitionSpec as P

BLOCK = 256
ITERS = 2


MIXING = 0.9
SHARPNESS = 3.0
EPSILON = 1e-06


def unit_rows(embeddings):
    values = embeddings.astype(jnp.float32)
    return (values * lax.rsqrt(jnp.sum(values * values, axis=1, keepdims=True) + EPSILON)).astype(
        jnp.bfloat16
    )


def symmetric_keep(tile_mask):
    blocks = tile_mask.shape[0]
    block_row = lax.broadcasted_iota(jnp.int32, (blocks, blocks), 0)
    block_col = lax.broadcasted_iota(jnp.int32, (blocks, blocks), 1)
    mirrored = jnp.where(block_row < block_col, tile_mask, tile_mask.T)
    return (jnp.where(block_row == block_col, 1, mirrored), block_row, block_col)


def rotate_rows(values, start):
    total = values.shape[0]
    doubled = jnp.concatenate([values, values], axis=0)
    return lax.dynamic_slice_in_dim(doubled, start, total, 0)


def one_term(operands):
    row_kernel, part_labels = operands
    return jnp.dot(row_kernel, part_labels, preferred_element_type=jnp.float32)


def no_term(operands):
    row_kernel, part_labels = operands
    return jnp.zeros((row_kernel.shape[0], part_labels.shape[1]), jnp.float32)


def shards(embeddings, labels, tile_mask):
    row_count = lax.axis_size("row")
    col_count = lax.axis_size("col")
    row_index = lax.axis_index("row")
    col_index = lax.axis_index("col")
    piece_rows = embeddings.shape[0]
    emb_width = embeddings.shape[1]
    channels = labels.shape[1]
    blocks = tile_mask.shape[0]
    sharpness = SHARPNESS * math.sqrt(emb_width)
    unit_vecs = unit_rows(embeddings)
    row_units = lax.all_gather(unit_vecs, "col", axis=0, tiled=True)
    col_gathered = lax.all_gather(unit_vecs, "row", axis=0, tiled=True)
    row_total = row_units.shape[0]
    col_total = col_gathered.shape[0]
    shift = row_index * piece_rows
    col_units = rotate_rows(col_gathered, shift)
    unit_count = math.gcd(8, row_count)
    unit_width = col_total // unit_count
    kept_sym, block_row, block_col = symmetric_keep(tile_mask)
    global_rows = row_index * row_total + jnp.arange(row_total, dtype=jnp.int32)
    row_blocks = global_rows // BLOCK
    block_ids = jnp.arange(blocks, dtype=jnp.int32)
    row_onehot = (row_blocks[:, None] == block_ids[None, :]).astype(jnp.bfloat16)
    row_table = jnp.dot(
        row_onehot, kept_sym.astype(jnp.bfloat16), preferred_element_type=jnp.float32
    ).astype(jnp.bfloat16)
    local_cols = (jnp.arange(col_total, dtype=jnp.int32) + shift) % col_total
    global_cols = (
        local_cols // piece_rows * col_count + col_index
    ) * piece_rows + local_cols % piece_rows
    col_blocks = global_cols // BLOCK
    kernels_row = []
    active_flags = []
    row_degree = jnp.zeros((row_total,), jnp.float32)
    for column_unit in range(unit_count):
        offset_cols = column_unit * unit_width
        part_units = col_units[offset_cols : offset_cols + unit_width]
        part_blocks = col_blocks[offset_cols : offset_cols + unit_width]
        part_cols = global_cols[offset_cols : offset_cols + unit_width]
        col_onehot = (part_blocks[:, None] == block_ids[None, :]).astype(jnp.bfloat16)
        kept_mask = lax.dot_general(
            row_table, col_onehot, (((1,), (1,)), ((), ())), preferred_element_type=jnp.float32
        )
        cosine = lax.dot_general(
            row_units, part_units, (((1,), (1,)), ((), ())), preferred_element_type=jnp.float32
        )
        distinct = global_rows[:, None] != part_cols[None, :]
        weights = jnp.where(
            distinct, jnp.exp(sharpness * cosine) * kept_mask, jnp.zeros_like(cosine)
        ).astype(jnp.bfloat16)
        active_flags.append(jnp.sum(kept_mask) > 0.0)
        kernels_row.append(weights)
        row_degree = row_degree + jnp.sum(weights, axis=1, dtype=jnp.float32)
    degree = lax.psum_scatter(row_degree, "col", scatter_dimension=0, tiled=True)
    inv_root = lax.rsqrt(degree)
    seed_scores = labels.astype(jnp.float32)
    current = seed_scores
    for iteration in range(ITERS):
        scaled = (inv_root[:, None] * current).astype(jnp.bfloat16)
        col_labels = rotate_rows(lax.all_gather(scaled, "row", axis=0, tiled=True), shift)
        row_sum = jnp.zeros((row_total, channels), jnp.float32)
        for column_unit in range(unit_count):
            offset_cols = column_unit * unit_width
            part_labels = col_labels[offset_cols : offset_cols + unit_width]
            row_sum = row_sum + lax.cond(
                active_flags[column_unit],
                one_term,
                no_term,
                (kernels_row[column_unit], part_labels),
            )
        sent_rows = row_sum.astype(jnp.bfloat16).reshape(col_count, piece_rows, channels)
        arrived = lax.all_to_all(sent_rows, "col", split_axis=0, concat_axis=0, tiled=True)
        spread = jnp.sum(arrived, axis=0, dtype=jnp.float32)
        current = MIXING * inv_root[:, None] * spread + (1.0 - MIXING) * seed_scores
    return current.astype(jnp.bfloat16)


AXES = ("row", "col")
CORES = 2
SHARE = 128
WHOLE_KERNEL_BYTES = 4 * 1024 * 1024
ROOM = 8 * 1024 * 1024


def chip_order(chips, team):
    first = chips // 2 + chips // 4 - 1
    return [first] + [chip for chip in range(chips) if chip != first]


def team_order(team):
    return list(range(team))[::-1]


def crossed(chip, chips):
    return int(chip >= chips // 2)


def pack_body(order, emb_hbm, lab_hbm, mask_hbm, sent_ref, kept_ref, emb_ref, lab_ref, sems):
    copies = [
        pltpu.make_async_copy(source, target, sems.at[k])
        for k, (source, target) in enumerate(
            ((emb_hbm, emb_ref), (lab_hbm, lab_ref), (mask_hbm, kept_ref))
        )
    ]
    for copy in copies:
        copy.start()
    peers, _, width = sent_ref.shape
    emb_width = emb_ref.shape[1]
    share = width - emb_width
    team = lab_ref.shape[1] // share
    copies[0].wait()
    unit_vecs = unit_rows(emb_ref[...])
    for peer in range(peers):
        sent_ref[peer, :, :emb_width] = unit_vecs
    copies[1].wait()
    for peer in range(peers):
        first = order[peer] % team * share
        sent_ref[peer, :, emb_width:] = lab_ref[:, first : first + share]
    copies[2].wait()


def block_runs(order, piece):
    runs = []
    for place, chip in enumerate(order):
        block = chip * CORES * piece // BLOCK
        if runs and runs[-1][2] == block:
            runs[-1][1] += piece
        else:
            runs.append([place * piece, (place + 1) * piece, block])
    return runs


def kernel_part(left, right, same, runs, kept_ref):
    sharpness = SHARPNESS * math.sqrt(left.shape[1])
    cosine = lax.dot_general(
        left, right, (((1,), (1,)), ((), ())), preferred_element_type=jnp.float32
    )
    weights = jnp.exp(sharpness * cosine)
    if same:
        row_ids = lax.broadcasted_iota(jnp.int32, weights.shape, 0)
        col_ids = lax.broadcasted_iota(jnp.int32, weights.shape, 1)
        weights = jnp.where(row_ids == col_ids, 0.0, weights)
    lines = []
    for row, row_end, i in runs:
        line = []
        for col, col_end, j in runs:
            part = weights[row:row_end, col:col_end]
            if i != j:
                low, high = min(i, j), max(i, j)
                part = part * kept_ref[low : low + 1, high : high + 1].astype(jnp.float32)
            line.append(part)
        lines.append(jnp.concatenate(line, axis=1))
    return jnp.concatenate(lines, axis=0).astype(jnp.bfloat16)


def mine_body(runs, emb_width, kept_ref, mine_ref, part_ref):
    mine = mine_ref[:, :emb_width]
    part_ref[...] = kernel_part(mine, mine, True, runs, kept_ref)


def spread_body(
    emb_width, order, ranks, runs, run_ref, kept_ref, part_ref, mine_ref, theirs_ref, out_ref, kernel_ref
):
    chips = len(order)
    team = len(ranks)
    half = mine_ref.shape[0]
    piece = half // chips
    share = out_ref.shape[1]
    units = (mine_ref[:, :emb_width], theirs_ref[:, :emb_width])
    ones = jnp.ones((half, share), jnp.bfloat16)
    degrees = []
    for s in range(2):
        degree = jnp.zeros((half, share), jnp.float32)
        for t in range(2):
            if s == 0 and t == 0:
                weights = part_ref[...]
            else:
                weights = kernel_part(units[s], units[t], s == t, runs, kept_ref)
            kernel_ref[s * half : (s + 1) * half, t * half : (t + 1) * half] = weights
            degree = degree + jnp.dot(weights, ones, preferred_element_type=jnp.float32)
        degrees.append(degree)
    labels = jnp.concatenate([mine_ref[:, emb_width:], theirs_ref[:, emb_width:]], axis=0).astype(
        jnp.float32
    )
    weights = kernel_ref[...]
    inv_root = lax.rsqrt(jnp.concatenate(degrees, axis=0))
    current = labels
    for iteration in range(ITERS - 1):
        scaled = (inv_root * current).astype(jnp.bfloat16)
        spread = jnp.dot(weights, scaled, preferred_element_type=jnp.float32)
        current = MIXING * inv_root * spread + (1.0 - MIXING) * labels
    scaled = (inv_root * current).astype(jnp.bfloat16)
    own = []
    for rank in ranks:
        place = jnp.int32(0)
        for run in range(chips // team):
            place = jnp.where(run_ref[0] == run, order.index(run * team + rank), place)
        own.append(pl.ds(pl.multiple_of(place * piece, 16), piece))
    own_weights = jnp.concatenate([kernel_ref[rows, :] for rows in own], axis=0)
    own_labels = jnp.concatenate([mine_ref[rows, emb_width:] for rows in own], axis=0)
    ones = jnp.ones((2 * half, share), jnp.bfloat16)
    own_root = lax.rsqrt(jnp.dot(own_weights, ones, preferred_element_type=jnp.float32))
    spread = jnp.dot(own_weights, scaled, preferred_element_type=jnp.float32)
    out_ref[...] = (
        MIXING * own_root * spread + (1.0 - MIXING) * own_labels.astype(jnp.float32)
    ).astype(jnp.bfloat16)


def whole_shards(embeddings, labels, tile_mask):
    piece_rows, emb_width = embeddings.shape
    channels = labels.shape[1]
    team = channels // SHARE
    devices = lax.axis_size(AXES)
    chips = devices // CORES
    half = chips * piece_rows
    width = emb_width + SHARE
    order = chip_order(chips, team)
    ranks = team_order(team)
    runs = block_runs(order, piece_rows)
    sides = [
        [chip * CORES + (side ^ crossed(chip, chips)) for chip in range(chips)]
        for side in range(CORES)
    ]
    gathered = [[side[chip] for chip in order] for side in sides]
    teams = [
        [side[first + rank] for rank in ranks] for first in range(0, chips, team) for side in sides
    ]
    vmem = pl.BlockSpec(memory_space=pltpu.VMEM)
    hbm = pl.BlockSpec(memory_space=pltpu.HBM)
    smem = pl.BlockSpec(memory_space=pltpu.SMEM)
    room = pltpu.CompilerParams(vmem_limit_bytes=ROOM)
    sent, kept = pl.pallas_call(
        functools.partial(pack_body, order),
        out_shape=(
            jax.ShapeDtypeStruct((chips, piece_rows, width), jnp.bfloat16),
            jax.ShapeDtypeStruct(tile_mask.shape, jnp.int32),
        ),
        in_specs=[hbm, hbm, hbm],
        out_specs=(vmem, vmem),
        scratch_shapes=[
            pltpu.VMEM(embeddings.shape, embeddings.dtype),
            pltpu.VMEM(labels.shape, labels.dtype),
            pltpu.SemaphoreType.DMA((3,)),
        ],
        compiler_params=room,
    )(*(pltpu.with_memory_space_constraint(x, pltpu.HBM) for x in (embeddings, labels, tile_mask)))
    mine = lax.all_to_all(
        sent, AXES, split_axis=0, concat_axis=0, axis_index_groups=gathered, tiled=True
    ).reshape(half, width)
    theirs = lax.ppermute(mine, AXES, [(i, i ^ 1) for i in range(devices)])
    part = pl.pallas_call(
        functools.partial(mine_body, runs, emb_width),
        out_shape=jax.ShapeDtypeStruct((half, half), jnp.bfloat16),
        in_specs=[vmem, vmem],
        out_specs=vmem,
        compiler_params=room,
        cost_estimate=pl.CostEstimate(
            flops=2 * half * half * emb_width,
            bytes_accessed=2 * half * (half + emb_width),
            transcendentals=half * half,
        ),
    )(kept, mine)
    run = (lax.axis_index(AXES) // (CORES * team)).astype(jnp.int32).reshape(1)
    team_out = pl.pallas_call(
        functools.partial(spread_body, emb_width, order, ranks, runs),
        out_shape=jax.ShapeDtypeStruct((team * piece_rows, SHARE), jnp.bfloat16),
        in_specs=[smem, vmem, vmem, vmem, vmem],
        out_specs=vmem,
        scratch_shapes=[pltpu.VMEM((2 * half, 2 * half), jnp.bfloat16)],
        compiler_params=room,
    )(run, kept, part, mine, theirs)
    pieces = lax.all_to_all(
        team_out.reshape(team, piece_rows, SHARE),
        AXES,
        split_axis=0,
        concat_axis=0,
        axis_index_groups=teams,
        tiled=True,
    )
    rows = jnp.stack([pieces[ranks.index(rank)] for rank in range(team)], axis=1)
    return rows.reshape(piece_rows, channels)


def solution(mesh):
    placed = (P(AXES, None), P(AXES, None), P())
    devices = mesh.devices.size

    def spread_labels(embeddings, labels, tile_mask):
        images = embeddings.shape[0]
        channels = labels.shape[1]
        whole = (
            images * images * 2 <= WHOLE_KERNEL_BYTES
            and images % (devices * 16) == 0
            and BLOCK % (images // devices * CORES) == 0
            and channels % SHARE == 0
            and devices % (channels // SHARE * CORES) == 0
        )
        return jax.shard_map(
            whole_shards if whole else shards,
            mesh=mesh,
            in_specs=placed,
            out_specs=P(AXES, None),
            check_vma=False,
        )(embeddings, labels, tile_mask)

    return spread_labels
```

```python
import functools
import math

import jax
import jax.numpy as jnp
from jax import lax
from jax.experimental import pallas as pl
from jax.experimental.pallas import tpu as pltpu
from jax.sharding import PartitionSpec as P

BLOCK = 256
ITERS = 2


MIXING = 0.9
SHARPNESS = 3.0
EPSILON = 1e-06


def unit_rows(embeddings):
    values = embeddings.astype(jnp.float32)
    return (values * lax.rsqrt(jnp.sum(values * values, axis=1, keepdims=True) + EPSILON)).astype(
        jnp.bfloat16
    )


def symmetric_keep(tile_mask):
    blocks = tile_mask.shape[0]
    block_row = lax.broadcasted_iota(jnp.int32, (blocks, blocks), 0)
    block_col = lax.broadcasted_iota(jnp.int32, (blocks, blocks), 1)
    mirrored = jnp.where(block_row < block_col, tile_mask, tile_mask.T)
    return (jnp.where(block_row == block_col, 1, mirrored), block_row, block_col)


def rotate_rows(values, start):
    total = values.shape[0]
    doubled = jnp.concatenate([values, values], axis=0)
    return lax.dynamic_slice_in_dim(doubled, start, total, 0)


def one_term(operands):
    row_kernel, part_labels = operands
    return jnp.dot(row_kernel, part_labels, preferred_element_type=jnp.float32)


def no_term(operands):
    row_kernel, part_labels = operands
    return jnp.zeros((row_kernel.shape[0], part_labels.shape[1]), jnp.float32)


def shards(embeddings, labels, tile_mask):
    row_count = lax.axis_size("row")
    col_count = lax.axis_size("col")
    row_index = lax.axis_index("row")
    col_index = lax.axis_index("col")
    piece_rows = embeddings.shape[0]
    emb_width = embeddings.shape[1]
    channels = labels.shape[1]
    blocks = tile_mask.shape[0]
    sharpness = SHARPNESS * math.sqrt(emb_width)
    unit_vecs = unit_rows(embeddings)
    row_units = lax.all_gather(unit_vecs, "col", axis=0, tiled=True)
    col_gathered = lax.all_gather(unit_vecs, "row", axis=0, tiled=True)
    row_total = row_units.shape[0]
    col_total = col_gathered.shape[0]
    shift = row_index * piece_rows
    col_units = rotate_rows(col_gathered, shift)
    unit_count = math.gcd(8, row_count)
    unit_width = col_total // unit_count
    kept_sym, block_row, block_col = symmetric_keep(tile_mask)
    global_rows = row_index * row_total + jnp.arange(row_total, dtype=jnp.int32)
    row_blocks = global_rows // BLOCK
    block_ids = jnp.arange(blocks, dtype=jnp.int32)
    row_onehot = (row_blocks[:, None] == block_ids[None, :]).astype(jnp.bfloat16)
    row_table = jnp.dot(
        row_onehot, kept_sym.astype(jnp.bfloat16), preferred_element_type=jnp.float32
    ).astype(jnp.bfloat16)
    local_cols = (jnp.arange(col_total, dtype=jnp.int32) + shift) % col_total
    global_cols = (
        local_cols // piece_rows * col_count + col_index
    ) * piece_rows + local_cols % piece_rows
    col_blocks = global_cols // BLOCK
    kernels_row = []
    active_flags = []
    row_degree = jnp.zeros((row_total,), jnp.float32)
    for column_unit in range(unit_count):
        offset_cols = column_unit * unit_width
        part_units = col_units[offset_cols : offset_cols + unit_width]
        part_blocks = col_blocks[offset_cols : offset_cols + unit_width]
        part_cols = global_cols[offset_cols : offset_cols + unit_width]
        col_onehot = (part_blocks[:, None] == block_ids[None, :]).astype(jnp.bfloat16)
        kept_mask = lax.dot_general(
            row_table, col_onehot, (((1,), (1,)), ((), ())), preferred_element_type=jnp.float32
        )
        cosine = lax.dot_general(
            row_units, part_units, (((1,), (1,)), ((), ())), preferred_element_type=jnp.float32
        )
        distinct = global_rows[:, None] != part_cols[None, :]
        weights = jnp.where(
            distinct, jnp.exp(sharpness * cosine) * kept_mask, jnp.zeros_like(cosine)
        ).astype(jnp.bfloat16)
        active_flags.append(jnp.sum(kept_mask) > 0.0)
        kernels_row.append(weights)
        row_degree = row_degree + jnp.sum(weights, axis=1, dtype=jnp.float32)
    degree = lax.psum_scatter(row_degree, "col", scatter_dimension=0, tiled=True)
    inv_root = lax.rsqrt(degree)
    seed_scores = labels.astype(jnp.float32)
    current = seed_scores
    for iteration in range(ITERS):
        scaled = (inv_root[:, None] * current).astype(jnp.bfloat16)
        col_labels = rotate_rows(lax.all_gather(scaled, "row", axis=0, tiled=True), shift)
        row_sum = jnp.zeros((row_total, channels), jnp.float32)
        for column_unit in range(unit_count):
            offset_cols = column_unit * unit_width
            part_labels = col_labels[offset_cols : offset_cols + unit_width]
            row_sum = row_sum + lax.cond(
                active_flags[column_unit],
                one_term,
                no_term,
                (kernels_row[column_unit], part_labels),
            )
        sent_rows = row_sum.astype(jnp.bfloat16).reshape(col_count, piece_rows, channels)
        arrived = lax.all_to_all(sent_rows, "col", split_axis=0, concat_axis=0, tiled=True)
        spread = jnp.sum(arrived, axis=0, dtype=jnp.float32)
        current = MIXING * inv_root[:, None] * spread + (1.0 - MIXING) * seed_scores
    return current.astype(jnp.bfloat16)


AXES = ("row", "col")
CORES = 2
SHARE = 128
WHOLE_KERNEL_BYTES = 4 * 1024 * 1024
ROOM = 8 * 1024 * 1024


def chip_order(chips):
    first = chips // 2 + chips // 4 - 1
    return [first] + [chip for chip in range(chips) if chip != first]


def team_order(team):
    return [team - 1] + list(range(team - 1))


def crossed(chip, chips):
    return int(0 < chip < chips // 2)


def pack_body(order, emb_hbm, lab_hbm, mask_hbm, sent_ref, kept_ref, emb_ref, lab_ref, sems):
    copies = [
        pltpu.make_async_copy(source, target, sems.at[k])
        for k, (source, target) in enumerate(
            ((emb_hbm, emb_ref), (lab_hbm, lab_ref), (mask_hbm, kept_ref))
        )
    ]
    for copy in copies:
        copy.start()
    peers, _, width = sent_ref.shape
    emb_width = emb_ref.shape[1]
    share = width - emb_width
    team = lab_ref.shape[1] // share
    copies[0].wait()
    unit_vecs = unit_rows(emb_ref[...])
    for peer in range(peers):
        sent_ref[peer, :, :emb_width] = unit_vecs
    copies[1].wait()
    for peer in range(peers):
        first = order[peer] % team * share
        sent_ref[peer, :, emb_width:] = lab_ref[:, first : first + share]
    copies[2].wait()


def block_runs(order, piece):
    runs = []
    for place, chip in enumerate(order):
        block = chip * CORES * piece // BLOCK
        if runs and runs[-1][2] == block:
            runs[-1][1] += piece
        else:
            runs.append([place * piece, (place + 1) * piece, block])
    return runs


def kernel_part(left, right, same, runs, kept_ref):
    sharpness = SHARPNESS * math.sqrt(left.shape[1])
    cosine = lax.dot_general(
        left, right, (((1,), (1,)), ((), ())), preferred_element_type=jnp.float32
    )
    weights = jnp.exp(sharpness * cosine)
    if same:
        row_ids = lax.broadcasted_iota(jnp.int32, weights.shape, 0)
        col_ids = lax.broadcasted_iota(jnp.int32, weights.shape, 1)
        weights = jnp.where(row_ids == col_ids, 0.0, weights)
    lines = []
    for row, row_end, i in runs:
        line = []
        for col, col_end, j in runs:
            part = weights[row:row_end, col:col_end]
            if i != j:
                low, high = min(i, j), max(i, j)
                part = part * kept_ref[low : low + 1, high : high + 1].astype(jnp.float32)
            line.append(part)
        lines.append(jnp.concatenate(line, axis=1))
    return jnp.concatenate(lines, axis=0).astype(jnp.bfloat16)


def row_sums(weights):
    return jnp.sum(weights.astype(jnp.float32), axis=1, keepdims=True)


def mine_body(runs, emb_width, kept_ref, mine_ref, part_ref, sums_ref):
    mine = mine_ref[:, :emb_width]
    weights = kernel_part(mine, mine, True, runs, kept_ref)
    part_ref[...] = weights
    sums_ref[...] = jnp.broadcast_to(row_sums(weights), sums_ref.shape)


def spread_body(
    emb_width, order, ranks, runs, run_ref, kept_ref, part_ref, sums_ref, mine_ref, theirs_ref, out_ref, kernel_ref, root_ref
):
    chips = len(order)
    team = len(ranks)
    half = mine_ref.shape[0]
    piece = half // chips
    share = out_ref.shape[1]
    units = (mine_ref[:, :emb_width], theirs_ref[:, :emb_width])
    kernel_ref[:half, :half] = part_ref[...]
    degrees = [sums_ref[...], jnp.zeros((half, 1), jnp.float32)]
    for s, t in ((0, 1), (1, 0), (1, 1)):
        weights = kernel_part(units[s], units[t], s == t, runs, kept_ref)
        kernel_ref[s * half : (s + 1) * half, t * half : (t + 1) * half] = weights
        degrees[s] = degrees[s] + row_sums(weights)
    degrees[1] = jnp.broadcast_to(degrees[1], (half, share))
    labels = jnp.concatenate([mine_ref[:, emb_width:], theirs_ref[:, emb_width:]], axis=0).astype(
        jnp.float32
    )
    weights = kernel_ref[...]
    inv_root = lax.rsqrt(jnp.concatenate(degrees, axis=0))
    root_ref[...] = inv_root[:half]
    current = labels
    for iteration in range(ITERS - 1):
        scaled = (inv_root * current).astype(jnp.bfloat16)
        spread = jnp.dot(weights, scaled, preferred_element_type=jnp.float32)
        current = MIXING * inv_root * spread + (1.0 - MIXING) * labels
    scaled = (inv_root * current).astype(jnp.bfloat16)
    own = []
    for rank in ranks:
        place = jnp.int32(0)
        for run in range(chips // team):
            place = jnp.where(run_ref[0] == run, order.index(run * team + rank), place)
        own.append(pl.ds(pl.multiple_of(place * piece, 16), piece))
    own_weights = jnp.concatenate([kernel_ref[rows, :] for rows in own], axis=0)
    own_labels = jnp.concatenate([mine_ref[rows, emb_width:] for rows in own], axis=0)
    own_root = jnp.concatenate([root_ref[rows, :] for rows in own], axis=0)
    spread = jnp.dot(own_weights, scaled, preferred_element_type=jnp.float32)
    out_ref[...] = (
        MIXING * own_root * spread + (1.0 - MIXING) * own_labels.astype(jnp.float32)
    ).astype(jnp.bfloat16)


def place_body(ranks, pieces_ref, out_ref):
    share = pieces_ref.shape[2]
    for place, rank in enumerate(ranks):
        out_ref[:, rank * share : (rank + 1) * share] = pieces_ref[place]


def whole_shards(embeddings, labels, tile_mask):
    piece_rows, emb_width = embeddings.shape
    channels = labels.shape[1]
    team = channels // SHARE
    devices = lax.axis_size(AXES)
    chips = devices // CORES
    half = chips * piece_rows
    width = emb_width + SHARE
    order = chip_order(chips)
    ranks = team_order(team)
    runs = block_runs(order, piece_rows)
    sides = [
        [chip * CORES + (side ^ crossed(chip, chips)) for chip in range(chips)]
        for side in range(CORES)
    ]
    gathered = [[side[chip] for chip in order] for side in sides]
    teams = [
        [side[first + rank] for rank in ranks] for first in range(0, chips, team) for side in sides
    ]
    vmem = pl.BlockSpec(memory_space=pltpu.VMEM)
    hbm = pl.BlockSpec(memory_space=pltpu.HBM)
    smem = pl.BlockSpec(memory_space=pltpu.SMEM)
    room = pltpu.CompilerParams(vmem_limit_bytes=ROOM)
    sent, kept = pl.pallas_call(
        functools.partial(pack_body, order),
        out_shape=(
            jax.ShapeDtypeStruct((chips, piece_rows, width), jnp.bfloat16),
            jax.ShapeDtypeStruct(tile_mask.shape, jnp.int32),
        ),
        in_specs=[hbm, hbm, hbm],
        out_specs=(vmem, vmem),
        scratch_shapes=[
            pltpu.VMEM(embeddings.shape, embeddings.dtype),
            pltpu.VMEM(labels.shape, labels.dtype),
            pltpu.SemaphoreType.DMA((3,)),
        ],
        compiler_params=room,
    )(*(pltpu.with_memory_space_constraint(x, pltpu.HBM) for x in (embeddings, labels, tile_mask)))
    mine = lax.all_to_all(
        sent, AXES, split_axis=0, concat_axis=0, axis_index_groups=gathered, tiled=True
    ).reshape(half, width)
    theirs = lax.ppermute(mine, AXES, [(i, i ^ 1) for i in range(devices)])
    part, sums = pl.pallas_call(
        functools.partial(mine_body, runs, emb_width),
        out_shape=(
            jax.ShapeDtypeStruct((half, half), jnp.bfloat16),
            jax.ShapeDtypeStruct((half, SHARE), jnp.float32),
        ),
        in_specs=[vmem, vmem],
        out_specs=(vmem, vmem),
        compiler_params=room,
        cost_estimate=pl.CostEstimate(
            flops=2 * half * half * emb_width,
            bytes_accessed=2 * half * (half + emb_width),
            transcendentals=half * half,
        ),
    )(kept, mine)
    run = (lax.axis_index(AXES) // (CORES * team)).astype(jnp.int32).reshape(1)
    team_out = pl.pallas_call(
        functools.partial(spread_body, emb_width, order, ranks, runs),
        out_shape=jax.ShapeDtypeStruct((team * piece_rows, SHARE), jnp.bfloat16),
        in_specs=[smem, vmem, vmem, vmem, vmem, vmem],
        out_specs=vmem,
        scratch_shapes=[
            pltpu.VMEM((2 * half, 2 * half), jnp.bfloat16),
            pltpu.VMEM((half, SHARE), jnp.float32),
        ],
        compiler_params=room,
    )(run, kept, part, sums, mine, theirs)
    pieces = lax.all_to_all(
        team_out.reshape(team, piece_rows, SHARE),
        AXES,
        split_axis=0,
        concat_axis=0,
        axis_index_groups=teams,
        tiled=True,
    )
    return pl.pallas_call(
        functools.partial(place_body, ranks),
        out_shape=jax.ShapeDtypeStruct((piece_rows, channels), jnp.bfloat16),
        in_specs=[vmem],
        out_specs=vmem,
        compiler_params=room,
    )(pieces)


def solution(mesh):
    placed = (P(AXES, None), P(AXES, None), P())
    devices = mesh.devices.size

    def spread_labels(embeddings, labels, tile_mask):
        images = embeddings.shape[0]
        channels = labels.shape[1]
        whole = (
            images * images * 2 <= WHOLE_KERNEL_BYTES
            and images % (devices * 16) == 0
            and BLOCK % (images // devices * CORES) == 0
            and channels % SHARE == 0
            and devices % (channels // SHARE * CORES) == 0
        )
        return jax.shard_map(
            whole_shards if whole else shards,
            mesh=mesh,
            in_specs=placed,
            out_specs=P(AXES, None),
            check_vma=False,
        )(embeddings, labels, tile_mask)

    return spread_labels
```

```python
import functools
import math

import jax
import jax.numpy as jnp
from jax import lax
from jax.experimental import pallas as pl
from jax.experimental.pallas import tpu as pltpu
from jax.sharding import PartitionSpec as P

BLOCK = 256
ITERS = 2


MIXING = 0.9
SHARPNESS = 3.0
EPSILON = 1e-06


def unit_rows(embeddings):
    values = embeddings.astype(jnp.float32)
    return (values * lax.rsqrt(jnp.sum(values * values, axis=1, keepdims=True) + EPSILON)).astype(
        jnp.bfloat16
    )


def symmetric_keep(tile_mask):
    blocks = tile_mask.shape[0]
    block_row = lax.broadcasted_iota(jnp.int32, (blocks, blocks), 0)
    block_col = lax.broadcasted_iota(jnp.int32, (blocks, blocks), 1)
    mirrored = jnp.where(block_row < block_col, tile_mask, tile_mask.T)
    return (jnp.where(block_row == block_col, 1, mirrored), block_row, block_col)


def rotate_rows(values, start):
    total = values.shape[0]
    doubled = jnp.concatenate([values, values], axis=0)
    return lax.dynamic_slice_in_dim(doubled, start, total, 0)


def one_term(operands):
    row_kernel, part_labels = operands
    return jnp.dot(row_kernel, part_labels, preferred_element_type=jnp.float32)


def no_term(operands):
    row_kernel, part_labels = operands
    return jnp.zeros((row_kernel.shape[0], part_labels.shape[1]), jnp.float32)


def shards(embeddings, labels, tile_mask):
    row_count = lax.axis_size("row")
    col_count = lax.axis_size("col")
    row_index = lax.axis_index("row")
    col_index = lax.axis_index("col")
    piece_rows = embeddings.shape[0]
    emb_width = embeddings.shape[1]
    channels = labels.shape[1]
    blocks = tile_mask.shape[0]
    sharpness = SHARPNESS * math.sqrt(emb_width)
    unit_vecs = unit_rows(embeddings)
    row_units = lax.all_gather(unit_vecs, "col", axis=0, tiled=True)
    col_gathered = lax.all_gather(unit_vecs, "row", axis=0, tiled=True)
    row_total = row_units.shape[0]
    col_total = col_gathered.shape[0]
    shift = row_index * piece_rows
    col_units = rotate_rows(col_gathered, shift)
    unit_count = math.gcd(8, row_count)
    unit_width = col_total // unit_count
    kept_sym, block_row, block_col = symmetric_keep(tile_mask)
    global_rows = row_index * row_total + jnp.arange(row_total, dtype=jnp.int32)
    row_blocks = global_rows // BLOCK
    block_ids = jnp.arange(blocks, dtype=jnp.int32)
    row_onehot = (row_blocks[:, None] == block_ids[None, :]).astype(jnp.bfloat16)
    row_table = jnp.dot(
        row_onehot, kept_sym.astype(jnp.bfloat16), preferred_element_type=jnp.float32
    ).astype(jnp.bfloat16)
    local_cols = (jnp.arange(col_total, dtype=jnp.int32) + shift) % col_total
    global_cols = (
        local_cols // piece_rows * col_count + col_index
    ) * piece_rows + local_cols % piece_rows
    col_blocks = global_cols // BLOCK
    kernels_row = []
    active_flags = []
    row_degree = jnp.zeros((row_total,), jnp.float32)
    for column_unit in range(unit_count):
        offset_cols = column_unit * unit_width
        part_units = col_units[offset_cols : offset_cols + unit_width]
        part_blocks = col_blocks[offset_cols : offset_cols + unit_width]
        part_cols = global_cols[offset_cols : offset_cols + unit_width]
        col_onehot = (part_blocks[:, None] == block_ids[None, :]).astype(jnp.bfloat16)
        kept_mask = lax.dot_general(
            row_table, col_onehot, (((1,), (1,)), ((), ())), preferred_element_type=jnp.float32
        )
        cosine = lax.dot_general(
            row_units, part_units, (((1,), (1,)), ((), ())), preferred_element_type=jnp.float32
        )
        distinct = global_rows[:, None] != part_cols[None, :]
        weights = jnp.where(
            distinct, jnp.exp(sharpness * cosine) * kept_mask, jnp.zeros_like(cosine)
        ).astype(jnp.bfloat16)
        active_flags.append(jnp.sum(kept_mask) > 0.0)
        kernels_row.append(weights)
        row_degree = row_degree + jnp.sum(weights, axis=1, dtype=jnp.float32)
    degree = lax.psum_scatter(row_degree, "col", scatter_dimension=0, tiled=True)
    inv_root = lax.rsqrt(degree)
    seed_scores = labels.astype(jnp.float32)
    current = seed_scores
    for iteration in range(ITERS):
        scaled = (inv_root[:, None] * current).astype(jnp.bfloat16)
        col_labels = rotate_rows(lax.all_gather(scaled, "row", axis=0, tiled=True), shift)
        row_sum = jnp.zeros((row_total, channels), jnp.float32)
        for column_unit in range(unit_count):
            offset_cols = column_unit * unit_width
            part_labels = col_labels[offset_cols : offset_cols + unit_width]
            row_sum = row_sum + lax.cond(
                active_flags[column_unit],
                one_term,
                no_term,
                (kernels_row[column_unit], part_labels),
            )
        sent_rows = row_sum.astype(jnp.bfloat16).reshape(col_count, piece_rows, channels)
        arrived = lax.all_to_all(sent_rows, "col", split_axis=0, concat_axis=0, tiled=True)
        spread = jnp.sum(arrived, axis=0, dtype=jnp.float32)
        current = MIXING * inv_root[:, None] * spread + (1.0 - MIXING) * seed_scores
    return current.astype(jnp.bfloat16)


AXES = ("row", "col")
CORES = 2
SHARE = 128
WHOLE_KERNEL_BYTES = 4 * 1024 * 1024
ROOM = 8 * 1024 * 1024


def chip_order(chips):
    first = chips // 2 + chips // 4 - 1
    return [first] + [chip for chip in range(chips) if chip != first]


def team_order(team):
    return [team - 1] + list(range(team - 1))


def gather_flip(chip, chips):
    return 1 * (chip >= chips // 2)


def team_flip(chip, chips):
    return 1 * (chip > 0) * (chip < chips // 2)


def pack_body(order, emb_hbm, lab_hbm, mask_hbm, sent_ref, kept_ref, emb_ref, lab_ref, sems):
    copies = [
        pltpu.make_async_copy(source, target, sems.at[k])
        for k, (source, target) in enumerate(
            ((emb_hbm, emb_ref), (lab_hbm, lab_ref), (mask_hbm, kept_ref))
        )
    ]
    for copy in copies:
        copy.start()
    peers, _, width = sent_ref.shape
    emb_width = emb_ref.shape[1]
    share = width - emb_width
    team = lab_ref.shape[1] // share
    copies[0].wait()
    unit_vecs = unit_rows(emb_ref[...])
    for peer in range(peers):
        sent_ref[peer, :, :emb_width] = unit_vecs
    copies[1].wait()
    for peer in range(peers):
        first = order[peer] % team * share
        sent_ref[peer, :, emb_width:] = lab_ref[:, first : first + share]
    copies[2].wait()


def block_runs(order, piece):
    runs = []
    for place, chip in enumerate(order):
        block = chip * CORES * piece // BLOCK
        if runs and runs[-1][2] == block:
            runs[-1][1] += piece
        else:
            runs.append([place * piece, (place + 1) * piece, block])
    return runs


def kernel_part(left, right, same, runs, kept_ref):
    sharpness = SHARPNESS * math.sqrt(left.shape[1])
    cosine = lax.dot_general(
        left, right, (((1,), (1,)), ((), ())), preferred_element_type=jnp.float32
    )
    weights = jnp.exp(sharpness * cosine)
    if same:
        row_ids = lax.broadcasted_iota(jnp.int32, weights.shape, 0)
        col_ids = lax.broadcasted_iota(jnp.int32, weights.shape, 1)
        weights = jnp.where(row_ids == col_ids, 0.0, weights)
    lines = []
    for row, row_end, i in runs:
        line = []
        for col, col_end, j in runs:
            part = weights[row:row_end, col:col_end]
            if i != j:
                low, high = min(i, j), max(i, j)
                part = part * kept_ref[low : low + 1, high : high + 1].astype(jnp.float32)
            line.append(part)
        lines.append(jnp.concatenate(line, axis=1))
    return jnp.concatenate(lines, axis=0).astype(jnp.bfloat16)


def row_sums(weights):
    return jnp.sum(weights.astype(jnp.float32), axis=1, keepdims=True)


def mine_body(runs, emb_width, kept_ref, mine_ref, part_ref, sums_ref):
    mine = mine_ref[:, :emb_width]
    weights = kernel_part(mine, mine, True, runs, kept_ref)
    part_ref[...] = weights
    sums_ref[...] = jnp.broadcast_to(row_sums(weights), sums_ref.shape)


def spread_body(
    emb_width, order, ranks, runs, rank_ref, kept_ref, part_ref, sums_ref, mine_ref, theirs_ref, out_ref, *scratch
):
    kernel_ref, root_ref, label_ref = scratch
    chips = len(order)
    team = len(ranks)
    half = mine_ref.shape[0]
    piece = half // chips
    share = out_ref.shape[1]
    units = (mine_ref[:, :emb_width], theirs_ref[:, :emb_width])
    kernel_ref[:half, :half] = part_ref[...]
    degrees = [sums_ref[...], jnp.zeros((half, 1), jnp.float32)]
    for s, t in ((0, 1), (1, 0), (1, 1)):
        weights = kernel_part(units[s], units[t], s == t, runs, kept_ref)
        kernel_ref[s * half : (s + 1) * half, t * half : (t + 1) * half] = weights
        degrees[s] = degrees[s] + row_sums(weights)
    degrees[1] = jnp.broadcast_to(degrees[1], (half, share))
    label_ref[:half] = mine_ref[:, emb_width:]
    label_ref[half:] = theirs_ref[:, emb_width:]
    labels = label_ref[...].astype(jnp.float32)
    weights = kernel_ref[...]
    inv_root = lax.rsqrt(jnp.concatenate(degrees, axis=0))
    root_ref[...] = inv_root
    current = labels
    for iteration in range(ITERS - 1):
        scaled = (inv_root * current).astype(jnp.bfloat16)
        spread = jnp.dot(weights, scaled, preferred_element_type=jnp.float32)
        current = MIXING * inv_root * spread + (1.0 - MIXING) * labels
    scaled = (inv_root * current).astype(jnp.bfloat16)
    chip, core = rank_ref[0] // CORES, rank_ref[0] % CORES
    gather_side = core ^ gather_flip(chip, chips)
    team_side = core ^ team_flip(chip, chips)
    own = []
    for rank in ranks:
        target = chip // team * team + rank
        side = team_side ^ team_flip(target, chips) ^ gather_flip(target, chips)
        place = jnp.where(target == order[0], 0, target + 1 * (target < order[0]))
        row = place * piece + half * (side ^ gather_side)
        own.append(pl.ds(pl.multiple_of(row, 16), piece))
    own_weights = jnp.concatenate([kernel_ref[rows, :] for rows in own], axis=0)
    own_labels = jnp.concatenate([label_ref[rows, :] for rows in own], axis=0)
    own_root = jnp.concatenate([root_ref[rows, :] for rows in own], axis=0)
    spread = jnp.dot(own_weights, scaled, preferred_element_type=jnp.float32)
    out_ref[...] = (
        MIXING * own_root * spread + (1.0 - MIXING) * own_labels.astype(jnp.float32)
    ).astype(jnp.bfloat16)


def place_body(ranks, pieces_ref, out_ref):
    share = pieces_ref.shape[2]
    for place, rank in enumerate(ranks):
        out_ref[:, rank * share : (rank + 1) * share] = pieces_ref[place]


def whole_shards(embeddings, labels, tile_mask):
    piece_rows, emb_width = embeddings.shape
    channels = labels.shape[1]
    team = channels // SHARE
    devices = lax.axis_size(AXES)
    chips = devices // CORES
    half = chips * piece_rows
    width = emb_width + SHARE
    order = chip_order(chips)
    ranks = team_order(team)
    runs = block_runs(order, piece_rows)
    gathered = [
        [chip * CORES + (side ^ gather_flip(chip, chips)) for chip in order]
        for side in range(CORES)
    ]
    teams = [
        [chip * CORES + (side ^ team_flip(chip, chips)) for chip in (first + rank for rank in ranks)]
        for first in range(0, chips, team)
        for side in range(CORES)
    ]
    vmem = pl.BlockSpec(memory_space=pltpu.VMEM)
    hbm = pl.BlockSpec(memory_space=pltpu.HBM)
    smem = pl.BlockSpec(memory_space=pltpu.SMEM)
    room = pltpu.CompilerParams(vmem_limit_bytes=ROOM)
    sent, kept = pl.pallas_call(
        functools.partial(pack_body, order),
        out_shape=(
            jax.ShapeDtypeStruct((chips, piece_rows, width), jnp.bfloat16),
            jax.ShapeDtypeStruct(tile_mask.shape, jnp.int32),
        ),
        in_specs=[hbm, hbm, hbm],
        out_specs=(vmem, vmem),
        scratch_shapes=[
            pltpu.VMEM(embeddings.shape, embeddings.dtype),
            pltpu.VMEM(labels.shape, labels.dtype),
            pltpu.SemaphoreType.DMA((3,)),
        ],
        compiler_params=room,
    )(*(pltpu.with_memory_space_constraint(x, pltpu.HBM) for x in (embeddings, labels, tile_mask)))
    mine = lax.all_to_all(
        sent, AXES, split_axis=0, concat_axis=0, axis_index_groups=gathered, tiled=True
    ).reshape(half, width)
    theirs = lax.ppermute(mine, AXES, [(i, i ^ 1) for i in range(devices)])
    part, sums = pl.pallas_call(
        functools.partial(mine_body, runs, emb_width),
        out_shape=(
            jax.ShapeDtypeStruct((half, half), jnp.bfloat16),
            jax.ShapeDtypeStruct((half, SHARE), jnp.float32),
        ),
        in_specs=[vmem, vmem],
        out_specs=(vmem, vmem),
        compiler_params=room,
        cost_estimate=pl.CostEstimate(
            flops=2 * half * half * emb_width,
            bytes_accessed=2 * half * (half + emb_width),
            transcendentals=half * half,
        ),
    )(kept, mine)
    rank = lax.axis_index(AXES).astype(jnp.int32).reshape(1)
    team_out = pl.pallas_call(
        functools.partial(spread_body, emb_width, order, ranks, runs),
        out_shape=jax.ShapeDtypeStruct((team * piece_rows, SHARE), jnp.bfloat16),
        in_specs=[smem, vmem, vmem, vmem, vmem, vmem],
        out_specs=vmem,
        scratch_shapes=[
            pltpu.VMEM((2 * half, 2 * half), jnp.bfloat16),
            pltpu.VMEM((2 * half, SHARE), jnp.float32),
            pltpu.VMEM((2 * half, SHARE), jnp.bfloat16),
        ],
        compiler_params=room,
    )(rank, kept, part, sums, mine, theirs)
    pieces = lax.all_to_all(
        team_out.reshape(team, piece_rows, SHARE),
        AXES,
        split_axis=0,
        concat_axis=0,
        axis_index_groups=teams,
        tiled=True,
    )
    return pl.pallas_call(
        functools.partial(place_body, ranks),
        out_shape=jax.ShapeDtypeStruct((piece_rows, channels), jnp.bfloat16),
        in_specs=[vmem],
        out_specs=vmem,
        compiler_params=room,
    )(pieces)


def solution(mesh):
    placed = (P(AXES, None), P(AXES, None), P())
    devices = mesh.devices.size

    def spread_labels(embeddings, labels, tile_mask):
        images = embeddings.shape[0]
        channels = labels.shape[1]
        whole = (
            images * images * 2 <= WHOLE_KERNEL_BYTES
            and images % (devices * 16) == 0
            and BLOCK % (images // devices * CORES) == 0
            and channels % SHARE == 0
            and devices % (channels // SHARE * CORES) == 0
        )
        return jax.shard_map(
            whole_shards if whole else shards,
            mesh=mesh,
            in_specs=placed,
            out_specs=P(AXES, None),
            check_vma=False,
        )(embeddings, labels, tile_mask)

    return spread_labels
```

```python
import functools
import math

import jax
import jax.numpy as jnp
from jax import lax
from jax.experimental import pallas as pl
from jax.experimental.pallas import tpu as pltpu
from jax.sharding import PartitionSpec as P

BLOCK = 256
ITERS = 2


MIXING = 0.9
SHARPNESS = 3.0
EPSILON = 1e-06


def unit_rows(embeddings):
    values = embeddings.astype(jnp.float32)
    return (values * lax.rsqrt(jnp.sum(values * values, axis=1, keepdims=True) + EPSILON)).astype(
        jnp.bfloat16
    )


def symmetric_keep(tile_mask):
    blocks = tile_mask.shape[0]
    block_row = lax.broadcasted_iota(jnp.int32, (blocks, blocks), 0)
    block_col = lax.broadcasted_iota(jnp.int32, (blocks, blocks), 1)
    mirrored = jnp.where(block_row < block_col, tile_mask, tile_mask.T)
    return (jnp.where(block_row == block_col, 1, mirrored), block_row, block_col)


def rotate_rows(values, start):
    total = values.shape[0]
    doubled = jnp.concatenate([values, values], axis=0)
    return lax.dynamic_slice_in_dim(doubled, start, total, 0)


def one_term(operands):
    row_kernel, part_labels = operands
    return jnp.dot(row_kernel, part_labels, preferred_element_type=jnp.float32)


def no_term(operands):
    row_kernel, part_labels = operands
    return jnp.zeros((row_kernel.shape[0], part_labels.shape[1]), jnp.float32)


def shards(embeddings, labels, tile_mask):
    row_count = lax.axis_size("row")
    col_count = lax.axis_size("col")
    row_index = lax.axis_index("row")
    col_index = lax.axis_index("col")
    piece_rows = embeddings.shape[0]
    emb_width = embeddings.shape[1]
    channels = labels.shape[1]
    blocks = tile_mask.shape[0]
    sharpness = SHARPNESS * math.sqrt(emb_width)
    unit_vecs = unit_rows(embeddings)
    row_units = lax.all_gather(unit_vecs, "col", axis=0, tiled=True)
    col_gathered = lax.all_gather(unit_vecs, "row", axis=0, tiled=True)
    row_total = row_units.shape[0]
    col_total = col_gathered.shape[0]
    shift = row_index * piece_rows
    col_units = rotate_rows(col_gathered, shift)
    unit_count = math.gcd(8, row_count)
    unit_width = col_total // unit_count
    kept_sym, block_row, block_col = symmetric_keep(tile_mask)
    global_rows = row_index * row_total + jnp.arange(row_total, dtype=jnp.int32)
    row_blocks = global_rows // BLOCK
    block_ids = jnp.arange(blocks, dtype=jnp.int32)
    row_onehot = (row_blocks[:, None] == block_ids[None, :]).astype(jnp.bfloat16)
    row_table = jnp.dot(
        row_onehot, kept_sym.astype(jnp.bfloat16), preferred_element_type=jnp.float32
    ).astype(jnp.bfloat16)
    local_cols = (jnp.arange(col_total, dtype=jnp.int32) + shift) % col_total
    global_cols = (
        local_cols // piece_rows * col_count + col_index
    ) * piece_rows + local_cols % piece_rows
    col_blocks = global_cols // BLOCK
    kernels_row = []
    active_flags = []
    row_degree = jnp.zeros((row_total,), jnp.float32)
    for column_unit in range(unit_count):
        offset_cols = column_unit * unit_width
        part_units = col_units[offset_cols : offset_cols + unit_width]
        part_blocks = col_blocks[offset_cols : offset_cols + unit_width]
        part_cols = global_cols[offset_cols : offset_cols + unit_width]
        col_onehot = (part_blocks[:, None] == block_ids[None, :]).astype(jnp.bfloat16)
        kept_mask = lax.dot_general(
            row_table, col_onehot, (((1,), (1,)), ((), ())), preferred_element_type=jnp.float32
        )
        cosine = lax.dot_general(
            row_units, part_units, (((1,), (1,)), ((), ())), preferred_element_type=jnp.float32
        )
        distinct = global_rows[:, None] != part_cols[None, :]
        weights = jnp.where(
            distinct, jnp.exp(sharpness * cosine) * kept_mask, jnp.zeros_like(cosine)
        ).astype(jnp.bfloat16)
        active_flags.append(jnp.sum(kept_mask) > 0.0)
        kernels_row.append(weights)
        row_degree = row_degree + jnp.sum(weights, axis=1, dtype=jnp.float32)
    degree = lax.psum_scatter(row_degree, "col", scatter_dimension=0, tiled=True)
    inv_root = lax.rsqrt(degree)
    seed_scores = labels.astype(jnp.float32)
    current = seed_scores
    for iteration in range(ITERS):
        scaled = (inv_root[:, None] * current).astype(jnp.bfloat16)
        col_labels = rotate_rows(lax.all_gather(scaled, "row", axis=0, tiled=True), shift)
        row_sum = jnp.zeros((row_total, channels), jnp.float32)
        for column_unit in range(unit_count):
            offset_cols = column_unit * unit_width
            part_labels = col_labels[offset_cols : offset_cols + unit_width]
            row_sum = row_sum + lax.cond(
                active_flags[column_unit],
                one_term,
                no_term,
                (kernels_row[column_unit], part_labels),
            )
        sent_rows = row_sum.astype(jnp.bfloat16).reshape(col_count, piece_rows, channels)
        arrived = lax.all_to_all(sent_rows, "col", split_axis=0, concat_axis=0, tiled=True)
        spread = jnp.sum(arrived, axis=0, dtype=jnp.float32)
        current = MIXING * inv_root[:, None] * spread + (1.0 - MIXING) * seed_scores
    return current.astype(jnp.bfloat16)


AXES = ("row", "col")
CORES = 2
SHARE = 128
WHOLE_KERNEL_BYTES = 4 * 1024 * 1024
ROOM = 8 * 1024 * 1024


def chip_order(chips):
    first = chips // 2 + chips // 4 - 1
    return [first] + [chip for chip in range(chips) if chip != first]


def team_order(team):
    return [team - 1] + list(range(team - 1))


def gather_flip(chip, chips):
    return 1 * (chip >= chips // 2)


def team_flip(chip, chips):
    return 1 * (chip > 0) * (chip < chips // 2)


def pack_body(order, emb_hbm, lab_hbm, mask_hbm, sent_ref, kept_ref, emb_ref, lab_ref, sems):
    copies = [
        pltpu.make_async_copy(source, target, sems.at[k])
        for k, (source, target) in enumerate(
            ((emb_hbm, emb_ref), (lab_hbm, lab_ref), (mask_hbm, kept_ref))
        )
    ]
    for copy in copies:
        copy.start()
    peers, _, width = sent_ref.shape
    emb_width = emb_ref.shape[1]
    share = width - emb_width
    team = lab_ref.shape[1] // share
    copies[0].wait()
    unit_vecs = unit_rows(emb_ref[...])
    for peer in range(peers):
        sent_ref[peer, :, :emb_width] = unit_vecs
    copies[1].wait()
    for peer in range(peers):
        first = order[peer] % team * share
        sent_ref[peer, :, emb_width:] = lab_ref[:, first : first + share]
    copies[2].wait()


def block_runs(order, piece):
    runs = []
    for place, chip in enumerate(order):
        block = chip * CORES * piece // BLOCK
        if runs and runs[-1][2] == block:
            runs[-1][1] += piece
        else:
            runs.append([place * piece, (place + 1) * piece, block])
    return runs


def kernel_part(left, right, same, runs, kept_ref):
    sharpness = SHARPNESS * math.sqrt(left.shape[1])
    cosine = lax.dot_general(
        left, right, (((1,), (1,)), ((), ())), preferred_element_type=jnp.float32
    )
    weights = jnp.exp(sharpness * cosine)
    if same:
        row_ids = lax.broadcasted_iota(jnp.int32, weights.shape, 0)
        col_ids = lax.broadcasted_iota(jnp.int32, weights.shape, 1)
        weights = jnp.where(row_ids == col_ids, 0.0, weights)
    lines = []
    for row, row_end, i in runs:
        line = []
        for col, col_end, j in runs:
            part = weights[row:row_end, col:col_end]
            if i != j:
                low, high = min(i, j), max(i, j)
                part = part * kept_ref[low : low + 1, high : high + 1].astype(jnp.float32)
            line.append(part)
        lines.append(jnp.concatenate(line, axis=1))
    return jnp.concatenate(lines, axis=0).astype(jnp.bfloat16)


def row_sums(weights):
    return jnp.sum(weights.astype(jnp.float32), axis=1, keepdims=True)


def mine_body(runs, emb_width, kept_ref, mine_ref, part_ref, sums_ref):
    mine = mine_ref[:, :emb_width]
    weights = kernel_part(mine, mine, True, runs, kept_ref)
    part_ref[...] = weights
    sums_ref[...] = jnp.broadcast_to(row_sums(weights), sums_ref.shape)


def spread_body(
    emb_width, order, ranks, runs, rank_ref, kept_ref, part_ref, sums_ref, mine_ref, theirs_ref, out_ref, *scratch
):
    kernel_ref, root_ref, label_ref = scratch
    chips = len(order)
    team = len(ranks)
    half = mine_ref.shape[0]
    piece = half // chips
    share = out_ref.shape[1]
    units = (mine_ref[:, :emb_width], theirs_ref[:, :emb_width])
    kernel_ref[:half, :half] = part_ref[...]
    degrees = [sums_ref[...], jnp.zeros((half, 1), jnp.float32)]
    across = kernel_part(units[0], units[1], False, runs, kept_ref)
    theirs = kernel_part(units[1], units[1], True, runs, kept_ref)
    back = across.T
    kernel_ref[:half, half:] = across
    kernel_ref[half:, :half] = back
    kernel_ref[half:, half:] = theirs
    degrees[0] = degrees[0] + row_sums(across)
    degrees[1] = jnp.broadcast_to(row_sums(back) + row_sums(theirs), (half, share))
    labels = jnp.concatenate([mine_ref[:, emb_width:], theirs_ref[:, emb_width:]], axis=0).astype(
        jnp.float32
    )
    weights = kernel_ref[...]
    inv_root = lax.rsqrt(jnp.concatenate(degrees, axis=0))
    root_ref[...] = MIXING * inv_root
    kept_part = (1.0 - MIXING) * labels
    label_ref[...] = kept_part
    current = labels
    for iteration in range(ITERS - 1):
        scaled = (inv_root * current).astype(jnp.bfloat16)
        spread = jnp.dot(weights, scaled, preferred_element_type=jnp.float32)
        current = MIXING * inv_root * spread + kept_part
    scaled = (inv_root * current).astype(jnp.bfloat16)
    chip, core = rank_ref[0] // CORES, rank_ref[0] % CORES
    gather_side = core ^ gather_flip(chip, chips)
    team_side = core ^ team_flip(chip, chips)
    own = []
    for rank in ranks:
        target = chip // team * team + rank
        side = team_side ^ team_flip(target, chips) ^ gather_flip(target, chips)
        place = jnp.where(target == order[0], 0, target + 1 * (target < order[0]))
        row = place * piece + half * (side ^ gather_side)
        own.append(pl.ds(pl.multiple_of(row, 16), piece))
    own_weights = jnp.concatenate([kernel_ref[rows, :] for rows in own], axis=0)
    own_labels = jnp.concatenate([label_ref[rows, :] for rows in own], axis=0)
    own_root = jnp.concatenate([root_ref[rows, :] for rows in own], axis=0)
    spread = jnp.dot(own_weights, scaled, preferred_element_type=jnp.float32)
    out_ref[...] = (own_root * spread + own_labels).astype(jnp.bfloat16)


def place_body(ranks, pieces_ref, out_ref):
    share = pieces_ref.shape[2]
    for place, rank in enumerate(ranks):
        out_ref[:, rank * share : (rank + 1) * share] = pieces_ref[place]


def whole_shards(embeddings, labels, tile_mask):
    piece_rows, emb_width = embeddings.shape
    channels = labels.shape[1]
    team = channels // SHARE
    devices = lax.axis_size(AXES)
    chips = devices // CORES
    half = chips * piece_rows
    width = emb_width + SHARE
    order = chip_order(chips)
    ranks = team_order(team)
    runs = block_runs(order, piece_rows)
    gathered = [
        [chip * CORES + (side ^ gather_flip(chip, chips)) for chip in order]
        for side in range(CORES)
    ]
    teams = [
        [chip * CORES + (side ^ team_flip(chip, chips)) for chip in (first + rank for rank in ranks)]
        for first in range(0, chips, team)
        for side in range(CORES)
    ]
    vmem = pl.BlockSpec(memory_space=pltpu.VMEM)
    hbm = pl.BlockSpec(memory_space=pltpu.HBM)
    smem = pl.BlockSpec(memory_space=pltpu.SMEM)
    room = pltpu.CompilerParams(vmem_limit_bytes=ROOM)
    sent, kept = pl.pallas_call(
        functools.partial(pack_body, order),
        out_shape=(
            jax.ShapeDtypeStruct((chips, piece_rows, width), jnp.bfloat16),
            jax.ShapeDtypeStruct(tile_mask.shape, jnp.int32),
        ),
        in_specs=[hbm, hbm, hbm],
        out_specs=(vmem, vmem),
        scratch_shapes=[
            pltpu.VMEM(embeddings.shape, embeddings.dtype),
            pltpu.VMEM(labels.shape, labels.dtype),
            pltpu.SemaphoreType.DMA((3,)),
        ],
        compiler_params=room,
    )(*(pltpu.with_memory_space_constraint(x, pltpu.HBM) for x in (embeddings, labels, tile_mask)))
    mine = lax.all_to_all(
        sent, AXES, split_axis=0, concat_axis=0, axis_index_groups=gathered, tiled=True
    ).reshape(half, width)
    theirs = lax.ppermute(mine, AXES, [(i, i ^ 1) for i in range(devices)])
    part, sums = pl.pallas_call(
        functools.partial(mine_body, runs, emb_width),
        out_shape=(
            jax.ShapeDtypeStruct((half, half), jnp.bfloat16),
            jax.ShapeDtypeStruct((half, SHARE), jnp.float32),
        ),
        in_specs=[vmem, vmem],
        out_specs=(vmem, vmem),
        compiler_params=room,
        cost_estimate=pl.CostEstimate(
            flops=2 * half * half * emb_width,
            bytes_accessed=2 * half * (half + emb_width),
            transcendentals=half * half,
        ),
    )(kept, mine)
    rank = lax.axis_index(AXES).astype(jnp.int32).reshape(1)
    team_out = pl.pallas_call(
        functools.partial(spread_body, emb_width, order, ranks, runs),
        out_shape=jax.ShapeDtypeStruct((team * piece_rows, SHARE), jnp.bfloat16),
        in_specs=[smem, vmem, vmem, vmem, vmem, vmem],
        out_specs=vmem,
        scratch_shapes=[
            pltpu.VMEM((2 * half, 2 * half), jnp.bfloat16),
            pltpu.VMEM((2 * half, SHARE), jnp.float32),
            pltpu.VMEM((2 * half, SHARE), jnp.float32),
        ],
        compiler_params=room,
    )(rank, kept, part, sums, mine, theirs)
    pieces = lax.all_to_all(
        team_out.reshape(team, piece_rows, SHARE),
        AXES,
        split_axis=0,
        concat_axis=0,
        axis_index_groups=teams,
        tiled=True,
    )
    return pl.pallas_call(
        functools.partial(place_body, ranks),
        out_shape=jax.ShapeDtypeStruct((piece_rows, channels), jnp.bfloat16),
        in_specs=[vmem],
        out_specs=vmem,
        compiler_params=room,
    )(pieces)


def solution(mesh):
    placed = (P(AXES, None), P(AXES, None), P())
    devices = mesh.devices.size

    def spread_labels(embeddings, labels, tile_mask):
        images = embeddings.shape[0]
        channels = labels.shape[1]
        whole = (
            images * images * 2 <= WHOLE_KERNEL_BYTES
            and images % (devices * 16) == 0
            and BLOCK % (images // devices * CORES) == 0
            and channels % SHARE == 0
            and devices % (channels // SHARE * CORES) == 0
        )
        return jax.shard_map(
            whole_shards if whole else shards,
            mesh=mesh,
            in_specs=placed,
            out_specs=P(AXES, None),
            check_vma=False,
        )(embeddings, labels, tile_mask)

    return spread_labels
```

```python
import functools
import math

import jax
import jax.numpy as jnp
from jax import lax
from jax.experimental import pallas as pl
from jax.experimental.pallas import tpu as pltpu
from jax.sharding import PartitionSpec as P

BLOCK = 256
ITERS = 2


MIXING = 0.9
SHARPNESS = 3.0
EPSILON = 1e-06


def unit_rows(embeddings):
    values = embeddings.astype(jnp.float32)
    return (values * lax.rsqrt(jnp.sum(values * values, axis=1, keepdims=True) + EPSILON)).astype(
        jnp.bfloat16
    )


def symmetric_keep(tile_mask):
    blocks = tile_mask.shape[0]
    block_row = lax.broadcasted_iota(jnp.int32, (blocks, blocks), 0)
    block_col = lax.broadcasted_iota(jnp.int32, (blocks, blocks), 1)
    mirrored = jnp.where(block_row < block_col, tile_mask, tile_mask.T)
    return (jnp.where(block_row == block_col, 1, mirrored), block_row, block_col)


def rotate_rows(values, start):
    total = values.shape[0]
    doubled = jnp.concatenate([values, values], axis=0)
    return lax.dynamic_slice_in_dim(doubled, start, total, 0)


def one_term(operands):
    row_kernel, part_labels = operands
    return jnp.dot(row_kernel, part_labels, preferred_element_type=jnp.float32)


def no_term(operands):
    row_kernel, part_labels = operands
    return jnp.zeros((row_kernel.shape[0], part_labels.shape[1]), jnp.float32)


def shards(embeddings, labels, tile_mask):
    row_count = lax.axis_size("row")
    col_count = lax.axis_size("col")
    row_index = lax.axis_index("row")
    col_index = lax.axis_index("col")
    piece_rows = embeddings.shape[0]
    emb_width = embeddings.shape[1]
    channels = labels.shape[1]
    blocks = tile_mask.shape[0]
    sharpness = SHARPNESS * math.sqrt(emb_width)
    unit_vecs = unit_rows(embeddings)
    row_units = lax.all_gather(unit_vecs, "col", axis=0, tiled=True)
    col_gathered = lax.all_gather(unit_vecs, "row", axis=0, tiled=True)
    row_total = row_units.shape[0]
    col_total = col_gathered.shape[0]
    shift = row_index * piece_rows
    col_units = rotate_rows(col_gathered, shift)
    unit_count = math.gcd(8, row_count)
    unit_width = col_total // unit_count
    kept_sym, block_row, block_col = symmetric_keep(tile_mask)
    global_rows = row_index * row_total + jnp.arange(row_total, dtype=jnp.int32)
    row_blocks = global_rows // BLOCK
    block_ids = jnp.arange(blocks, dtype=jnp.int32)
    row_onehot = (row_blocks[:, None] == block_ids[None, :]).astype(jnp.bfloat16)
    row_table = jnp.dot(
        row_onehot, kept_sym.astype(jnp.bfloat16), preferred_element_type=jnp.float32
    ).astype(jnp.bfloat16)
    local_cols = (jnp.arange(col_total, dtype=jnp.int32) + shift) % col_total
    global_cols = (
        local_cols // piece_rows * col_count + col_index
    ) * piece_rows + local_cols % piece_rows
    col_blocks = global_cols // BLOCK
    kernels_row = []
    active_flags = []
    row_degree = jnp.zeros((row_total,), jnp.float32)
    for column_unit in range(unit_count):
        offset_cols = column_unit * unit_width
        part_units = col_units[offset_cols : offset_cols + unit_width]
        part_blocks = col_blocks[offset_cols : offset_cols + unit_width]
        part_cols = global_cols[offset_cols : offset_cols + unit_width]
        col_onehot = (part_blocks[:, None] == block_ids[None, :]).astype(jnp.bfloat16)
        kept_mask = lax.dot_general(
            row_table, col_onehot, (((1,), (1,)), ((), ())), preferred_element_type=jnp.float32
        )
        cosine = lax.dot_general(
            row_units, part_units, (((1,), (1,)), ((), ())), preferred_element_type=jnp.float32
        )
        distinct = global_rows[:, None] != part_cols[None, :]
        weights = jnp.where(
            distinct, jnp.exp(sharpness * cosine) * kept_mask, jnp.zeros_like(cosine)
        ).astype(jnp.bfloat16)
        active_flags.append(jnp.sum(kept_mask) > 0.0)
        kernels_row.append(weights)
        row_degree = row_degree + jnp.sum(weights, axis=1, dtype=jnp.float32)
    degree = lax.psum_scatter(row_degree, "col", scatter_dimension=0, tiled=True)
    inv_root = lax.rsqrt(degree)
    seed_scores = labels.astype(jnp.float32)
    current = seed_scores
    for iteration in range(ITERS):
        scaled = (inv_root[:, None] * current).astype(jnp.bfloat16)
        col_labels = rotate_rows(lax.all_gather(scaled, "row", axis=0, tiled=True), shift)
        row_sum = jnp.zeros((row_total, channels), jnp.float32)
        for column_unit in range(unit_count):
            offset_cols = column_unit * unit_width
            part_labels = col_labels[offset_cols : offset_cols + unit_width]
            row_sum = row_sum + lax.cond(
                active_flags[column_unit],
                one_term,
                no_term,
                (kernels_row[column_unit], part_labels),
            )
        sent_rows = row_sum.astype(jnp.bfloat16).reshape(col_count, piece_rows, channels)
        arrived = lax.all_to_all(sent_rows, "col", split_axis=0, concat_axis=0, tiled=True)
        spread = jnp.sum(arrived, axis=0, dtype=jnp.float32)
        current = MIXING * inv_root[:, None] * spread + (1.0 - MIXING) * seed_scores
    return current.astype(jnp.bfloat16)


AXES = ("row", "col")
CORES = 2
SHARE = 512
LANES = 128
WHOLE_KERNEL_BYTES = 4 * 1024 * 1024
ROOM = 8 * 1024 * 1024


def chip_order(chips):
    first = chips // 2 + chips // 4 - 1
    return [first] + [chip for chip in range(chips) if chip != first]


def gather_flip(chip, chips):
    return 1 * (chip >= chips // 2)


def pack_body(order, emb_hbm, lab_hbm, mask_hbm, sent_ref, kept_ref, emb_ref, lab_ref, sems):
    copies = [
        pltpu.make_async_copy(source, target, sems.at[k])
        for k, (source, target) in enumerate(
            ((emb_hbm, emb_ref), (lab_hbm, lab_ref), (mask_hbm, kept_ref))
        )
    ]
    for copy in copies:
        copy.start()
    peers, _, width = sent_ref.shape
    emb_width = emb_ref.shape[1]
    share = width - emb_width
    team = lab_ref.shape[1] // share
    copies[0].wait()
    unit_vecs = unit_rows(emb_ref[...])
    for peer in range(peers):
        sent_ref[peer, :, :emb_width] = unit_vecs
    copies[1].wait()
    for peer in range(peers):
        first = order[peer] % team * share
        sent_ref[peer, :, emb_width:] = lab_ref[:, first : first + share]
    copies[2].wait()


def block_runs(order, piece):
    runs = []
    for place, chip in enumerate(order):
        block = chip * CORES * piece // BLOCK
        if runs and runs[-1][2] == block:
            runs[-1][1] += piece
        else:
            runs.append([place * piece, (place + 1) * piece, block])
    return runs


def kernel_part(left, right, same, runs, kept_ref):
    sharpness = SHARPNESS * math.sqrt(left.shape[1])
    cosine = lax.dot_general(
        left, right, (((1,), (1,)), ((), ())), preferred_element_type=jnp.float32
    )
    weights = jnp.exp(sharpness * cosine)
    if same:
        row_ids = lax.broadcasted_iota(jnp.int32, weights.shape, 0)
        col_ids = lax.broadcasted_iota(jnp.int32, weights.shape, 1)
        weights = jnp.where(row_ids == col_ids, 0.0, weights)
    lines = []
    for row, row_end, i in runs:
        line = []
        for col, col_end, j in runs:
            part = weights[row:row_end, col:col_end]
            if i != j:
                low, high = min(i, j), max(i, j)
                part = part * kept_ref[low : low + 1, high : high + 1].astype(jnp.float32)
            line.append(part)
        lines.append(jnp.concatenate(line, axis=1))
    return jnp.concatenate(lines, axis=0).astype(jnp.bfloat16)


def row_sums(weights):
    return jnp.sum(weights.astype(jnp.float32), axis=1, keepdims=True)


def mine_body(runs, emb_width, kept_ref, mine_ref, part_ref, sums_ref):
    mine = mine_ref[:, :emb_width]
    weights = kernel_part(mine, mine, True, runs, kept_ref)
    part_ref[...] = weights
    sums_ref[...] = jnp.broadcast_to(row_sums(weights), sums_ref.shape)


def own_place(rank, order, step, piece):
    chips = len(order)
    chip, core = rank // CORES, rank % CORES
    target = chip ^ step
    place = jnp.where(target == order[0], 0, target + 1 * (target < order[0]))
    other = gather_flip(chip, chips) ^ gather_flip(target, chips) ^ min(step, 1)
    return pl.multiple_of(place * piece, 16), other


def whole_body(
    order, team, runs, emb_width, rank_ref, kept_ref, part_ref, sums_ref, mine_ref, start_ref, *rest
):
    steps_ref, root_ref, kernel_ref = rest
    half = mine_ref.shape[0]
    piece = half // len(order)
    units = (mine_ref[:, :emb_width], start_ref[:, :emb_width])
    kernel_ref[:half, :half] = part_ref[...]
    across = kernel_part(units[0], units[1], False, runs, kept_ref)
    theirs = kernel_part(units[1], units[1], True, runs, kept_ref)
    back = across.T
    kernel_ref[:half, half:] = across
    kernel_ref[half:, :half] = back
    kernel_ref[half:, half:] = theirs
    degree = sums_ref[...] + row_sums(across)
    roots = lax.rsqrt(
        jnp.concatenate(
            [degree, jnp.broadcast_to(row_sums(back) + row_sums(theirs), degree.shape)], axis=0
        )
    )
    root_ref[...] = roots
    weights = kernel_ref[...].astype(jnp.float32)
    shares = jnp.concatenate([roots * roots] * (2 * half // LANES), axis=1)
    passed = (shares * weights).astype(jnp.bfloat16)
    own = []
    for step in range(team):
        place, other = own_place(rank_ref[0], order, step, piece)
        own.append(kernel_ref[pl.ds(pl.multiple_of(place + half * other, 16), piece), :])
    first = MIXING * jnp.concatenate(own, axis=0).astype(jnp.float32)
    steps = first
    for iteration in range(ITERS - 1):
        steps = MIXING * jnp.dot(
            steps.astype(jnp.bfloat16), passed, preferred_element_type=jnp.float32
        ) + (1.0 - MIXING) * first
    steps_ref[...] = steps.astype(jnp.bfloat16)


def spread_body(emb_width, order, rank_ref, steps_ref, root_ref, mine_ref, start_ref, end_ref, *out_refs):
    half = mine_ref.shape[0]
    share = mine_ref.shape[1] - emb_width
    piece = half // len(order)
    theirs = jnp.concatenate([start_ref[:, emb_width:], end_ref[...]], axis=1)
    labels = jnp.concatenate([mine_ref[:, emb_width:], theirs], axis=0).astype(jnp.float32)
    inv_root = jnp.concatenate([root_ref[...]] * (share // LANES), axis=1)
    scaled = (inv_root * labels).astype(jnp.bfloat16)
    spread = jnp.dot(steps_ref[...], scaled, preferred_element_type=jnp.float32)
    for step, out_ref in enumerate(out_refs):
        place, other = own_place(rank_ref[0], order, step, piece)
        rows = pl.ds(place, piece)
        root = root_ref[pl.ds(pl.multiple_of(place + half * other, 16), piece), :]
        root = jnp.concatenate([root] * (share // LANES), axis=1)
        theirs = jnp.concatenate([start_ref[rows, emb_width:], end_ref[rows, :]], axis=1)
        own = jnp.where(
            other == 0, mine_ref[rows, emb_width:].astype(jnp.float32), theirs.astype(jnp.float32)
        )
        out_ref[...] = (
            root * spread[step * piece : (step + 1) * piece] + (1.0 - MIXING) * own
        ).astype(jnp.bfloat16)


def place_body(rank_ref, *refs):
    pieces, out_ref = refs[:-1], refs[-1]
    share = pieces[0].shape[1]
    chip = rank_ref[0] // CORES
    for step, piece_ref in enumerate(pieces):
        first = pl.multiple_of((chip ^ step) % len(pieces) * share, LANES)
        out_ref[:, pl.ds(first, share)] = piece_ref[...]


def whole_shards(embeddings, labels, tile_mask):
    piece_rows, emb_width = embeddings.shape
    channels = labels.shape[1]
    team = channels // SHARE
    devices = lax.axis_size(AXES)
    chips = devices // CORES
    half = chips * piece_rows
    width = emb_width + SHARE
    order = chip_order(chips)
    runs = block_runs(order, piece_rows)
    gathered = [
        [chip * CORES + (side ^ gather_flip(chip, chips)) for chip in order]
        for side in range(CORES)
    ]
    vmem = pl.BlockSpec(memory_space=pltpu.VMEM)
    hbm = pl.BlockSpec(memory_space=pltpu.HBM)
    smem = pl.BlockSpec(memory_space=pltpu.SMEM)
    room = pltpu.CompilerParams(vmem_limit_bytes=ROOM)
    sent, kept = pl.pallas_call(
        functools.partial(pack_body, order),
        out_shape=(
            jax.ShapeDtypeStruct((chips, piece_rows, width), jnp.bfloat16),
            jax.ShapeDtypeStruct(tile_mask.shape, jnp.int32),
        ),
        in_specs=[hbm, hbm, hbm],
        out_specs=(vmem, vmem),
        scratch_shapes=[
            pltpu.VMEM(embeddings.shape, embeddings.dtype),
            pltpu.VMEM(labels.shape, labels.dtype),
            pltpu.SemaphoreType.DMA((3,)),
        ],
        compiler_params=room,
    )(*(pltpu.with_memory_space_constraint(x, pltpu.HBM) for x in (embeddings, labels, tile_mask)))
    mine = lax.all_to_all(
        sent, AXES, split_axis=0, concat_axis=0, axis_index_groups=gathered, tiled=True
    ).reshape(half, width)
    swap = [(i, i ^ 1) for i in range(devices)]
    middle = width // 2
    their_start = lax.ppermute(mine[:, :middle], AXES, swap)
    their_end = lax.ppermute(mine[:, middle:], AXES, swap)
    part, sums = pl.pallas_call(
        functools.partial(mine_body, runs, emb_width),
        out_shape=(
            jax.ShapeDtypeStruct((half, half), jnp.bfloat16),
            jax.ShapeDtypeStruct((half, LANES), jnp.float32),
        ),
        in_specs=[vmem, vmem],
        out_specs=(vmem, vmem),
        compiler_params=room,
        cost_estimate=pl.CostEstimate(
            flops=2 * half * half * emb_width,
            bytes_accessed=2 * half * (half + emb_width),
            transcendentals=half * half,
        ),
    )(kept, mine)
    rank = lax.axis_index(AXES).astype(jnp.int32).reshape(1)
    steps, root = pl.pallas_call(
        functools.partial(whole_body, order, team, runs, emb_width),
        out_shape=(
            jax.ShapeDtypeStruct((team * piece_rows, 2 * half), jnp.bfloat16),
            jax.ShapeDtypeStruct((2 * half, LANES), jnp.float32),
        ),
        in_specs=[smem] + [vmem] * 5,
        out_specs=(vmem, vmem),
        scratch_shapes=[pltpu.VMEM((2 * half, 2 * half), jnp.bfloat16)],
        compiler_params=room,
        cost_estimate=pl.CostEstimate(
            flops=4 * half * half * emb_width,
            bytes_accessed=8 * half * half,
            transcendentals=2 * half * half,
        ),
    )(rank, kept, part, sums, mine, their_start)
    piece = jax.ShapeDtypeStruct((piece_rows, SHARE), jnp.bfloat16)
    kept_piece, *sent_pieces = pl.pallas_call(
        functools.partial(spread_body, emb_width, order),
        out_shape=(piece,) * team,
        in_specs=[smem] + [vmem] * 5,
        out_specs=(vmem,) * team,
        compiler_params=room,
    )(rank, steps, root, mine, their_start, their_end)
    pieces = [kept_piece] + [
        lax.ppermute(sent_piece, AXES, [(i, i ^ (CORES * step + 1)) for i in range(devices)])
        for step, sent_piece in enumerate(sent_pieces, 1)
    ]
    return pl.pallas_call(
        place_body,
        out_shape=jax.ShapeDtypeStruct((piece_rows, channels), jnp.bfloat16),
        in_specs=[smem] + [vmem] * team,
        out_specs=vmem,
        compiler_params=room,
    )(rank, *pieces)


def solution(mesh):
    placed = (P(AXES, None), P(AXES, None), P())
    devices = mesh.devices.size

    def spread_labels(embeddings, labels, tile_mask):
        images = embeddings.shape[0]
        channels = labels.shape[1]
        whole = (
            images * images * 2 <= WHOLE_KERNEL_BYTES
            and images % (devices * 16) == 0
            and BLOCK % (images // devices * CORES) == 0
            and channels % SHARE == 0
            and devices % (channels // SHARE * CORES) == 0
            and (channels // SHARE) & (channels // SHARE - 1) == 0
        )
        return jax.shard_map(
            whole_shards if whole else shards,
            mesh=mesh,
            in_specs=placed,
            out_specs=P(AXES, None),
            check_vma=False,
        )(embeddings, labels, tile_mask)

    return spread_labels
```

```python
import functools
import math

import jax
import jax.numpy as jnp
from jax import lax
from jax.experimental import pallas as pl
from jax.experimental.pallas import tpu as pltpu
from jax.sharding import PartitionSpec as P

BLOCK = 256
ITERS = 2


MIXING = 0.9
SHARPNESS = 3.0
EPSILON = 1e-06


def unit_rows(embeddings):
    values = embeddings.astype(jnp.float32)
    return (values * lax.rsqrt(jnp.sum(values * values, axis=1, keepdims=True) + EPSILON)).astype(
        jnp.bfloat16
    )


def symmetric_keep(tile_mask):
    blocks = tile_mask.shape[0]
    block_row = lax.broadcasted_iota(jnp.int32, (blocks, blocks), 0)
    block_col = lax.broadcasted_iota(jnp.int32, (blocks, blocks), 1)
    mirrored = jnp.where(block_row < block_col, tile_mask, tile_mask.T)
    return (jnp.where(block_row == block_col, 1, mirrored), block_row, block_col)


def rotate_rows(values, start):
    total = values.shape[0]
    doubled = jnp.concatenate([values, values], axis=0)
    return lax.dynamic_slice_in_dim(doubled, start, total, 0)


def one_term(operands):
    row_kernel, part_labels = operands
    return jnp.dot(row_kernel, part_labels, preferred_element_type=jnp.float32)


def no_term(operands):
    row_kernel, part_labels = operands
    return jnp.zeros((row_kernel.shape[0], part_labels.shape[1]), jnp.float32)


def shards(embeddings, labels, tile_mask):
    row_count = lax.axis_size("row")
    col_count = lax.axis_size("col")
    row_index = lax.axis_index("row")
    col_index = lax.axis_index("col")
    piece_rows = embeddings.shape[0]
    emb_width = embeddings.shape[1]
    channels = labels.shape[1]
    blocks = tile_mask.shape[0]
    sharpness = SHARPNESS * math.sqrt(emb_width)
    unit_vecs = unit_rows(embeddings)
    row_units = lax.all_gather(unit_vecs, "col", axis=0, tiled=True)
    col_gathered = lax.all_gather(unit_vecs, "row", axis=0, tiled=True)
    row_total = row_units.shape[0]
    col_total = col_gathered.shape[0]
    shift = row_index * piece_rows
    col_units = rotate_rows(col_gathered, shift)
    unit_count = math.gcd(8, row_count)
    unit_width = col_total // unit_count
    kept_sym, block_row, block_col = symmetric_keep(tile_mask)
    global_rows = row_index * row_total + jnp.arange(row_total, dtype=jnp.int32)
    row_blocks = global_rows // BLOCK
    block_ids = jnp.arange(blocks, dtype=jnp.int32)
    row_onehot = (row_blocks[:, None] == block_ids[None, :]).astype(jnp.bfloat16)
    row_table = jnp.dot(
        row_onehot, kept_sym.astype(jnp.bfloat16), preferred_element_type=jnp.float32
    ).astype(jnp.bfloat16)
    local_cols = (jnp.arange(col_total, dtype=jnp.int32) + shift) % col_total
    global_cols = (
        local_cols // piece_rows * col_count + col_index
    ) * piece_rows + local_cols % piece_rows
    col_blocks = global_cols // BLOCK
    kernels_row = []
    active_flags = []
    row_degree = jnp.zeros((row_total,), jnp.float32)
    for column_unit in range(unit_count):
        offset_cols = column_unit * unit_width
        part_units = col_units[offset_cols : offset_cols + unit_width]
        part_blocks = col_blocks[offset_cols : offset_cols + unit_width]
        part_cols = global_cols[offset_cols : offset_cols + unit_width]
        col_onehot = (part_blocks[:, None] == block_ids[None, :]).astype(jnp.bfloat16)
        kept_mask = lax.dot_general(
            row_table, col_onehot, (((1,), (1,)), ((), ())), preferred_element_type=jnp.float32
        )
        cosine = lax.dot_general(
            row_units, part_units, (((1,), (1,)), ((), ())), preferred_element_type=jnp.float32
        )
        distinct = global_rows[:, None] != part_cols[None, :]
        weights = jnp.where(
            distinct, jnp.exp(sharpness * cosine) * kept_mask, jnp.zeros_like(cosine)
        ).astype(jnp.bfloat16)
        active_flags.append(jnp.sum(kept_mask) > 0.0)
        kernels_row.append(weights)
        row_degree = row_degree + jnp.sum(weights, axis=1, dtype=jnp.float32)
    degree = lax.psum_scatter(row_degree, "col", scatter_dimension=0, tiled=True)
    inv_root = lax.rsqrt(degree)
    seed_scores = labels.astype(jnp.float32)
    current = seed_scores
    for iteration in range(ITERS):
        scaled = (inv_root[:, None] * current).astype(jnp.bfloat16)
        col_labels = rotate_rows(lax.all_gather(scaled, "row", axis=0, tiled=True), shift)
        row_sum = jnp.zeros((row_total, channels), jnp.float32)
        for column_unit in range(unit_count):
            offset_cols = column_unit * unit_width
            part_labels = col_labels[offset_cols : offset_cols + unit_width]
            row_sum = row_sum + lax.cond(
                active_flags[column_unit],
                one_term,
                no_term,
                (kernels_row[column_unit], part_labels),
            )
        sent_rows = row_sum.astype(jnp.bfloat16).reshape(col_count, piece_rows, channels)
        arrived = lax.all_to_all(sent_rows, "col", split_axis=0, concat_axis=0, tiled=True)
        spread = jnp.sum(arrived, axis=0, dtype=jnp.float32)
        current = MIXING * inv_root[:, None] * spread + (1.0 - MIXING) * seed_scores
    return current.astype(jnp.bfloat16)


AXES = ("row", "col")
CORES = 2
SHARE = 128
WHOLE_KERNEL_BYTES = 4 * 1024 * 1024
ROOM = 8 * 1024 * 1024


def chip_order(chips):
    first = chips // 2 + chips // 4 - 1
    return [first] + [chip for chip in range(chips) if chip != first]


def team_order(team):
    return [team - 1] + list(range(team - 1))


def gather_flip(chip, chips):
    return 1 * (chip >= chips // 2)


def team_flip(chip, chips):
    return 1 * (chip > 0) * (chip < chips // 2)


def pack_body(order, emb_hbm, lab_hbm, mask_hbm, sent_ref, kept_ref, emb_ref, lab_ref, sems):
    copies = [
        pltpu.make_async_copy(source, target, sems.at[k])
        for k, (source, target) in enumerate(
            ((emb_hbm, emb_ref), (lab_hbm, lab_ref), (mask_hbm, kept_ref))
        )
    ]
    for copy in copies:
        copy.start()
    peers, _, width = sent_ref.shape
    emb_width = emb_ref.shape[1]
    share = width - emb_width
    team = lab_ref.shape[1] // share
    copies[0].wait()
    unit_vecs = unit_rows(emb_ref[...])
    for peer in range(peers):
        sent_ref[peer, :, :emb_width] = unit_vecs
    copies[1].wait()
    for peer in range(peers):
        first = order[peer] % team * share
        sent_ref[peer, :, emb_width:] = lab_ref[:, first : first + share]
    copies[2].wait()


def block_runs(order, piece):
    runs = []
    for place, chip in enumerate(order):
        block = chip * CORES * piece // BLOCK
        if runs and runs[-1][2] == block:
            runs[-1][1] += piece
        else:
            runs.append([place * piece, (place + 1) * piece, block])
    return runs


def kernel_part(left, right, same, runs, kept_ref):
    sharpness = SHARPNESS * math.sqrt(left.shape[1])
    cosine = lax.dot_general(
        left, right, (((1,), (1,)), ((), ())), preferred_element_type=jnp.float32
    )
    weights = jnp.exp(sharpness * cosine)
    if same:
        row_ids = lax.broadcasted_iota(jnp.int32, weights.shape, 0)
        col_ids = lax.broadcasted_iota(jnp.int32, weights.shape, 1)
        weights = jnp.where(row_ids == col_ids, 0.0, weights)
    lines = []
    for row, row_end, i in runs:
        line = []
        for col, col_end, j in runs:
            part = weights[row:row_end, col:col_end]
            if i != j:
                low, high = min(i, j), max(i, j)
                part = part * kept_ref[low : low + 1, high : high + 1].astype(jnp.float32)
            line.append(part)
        lines.append(jnp.concatenate(line, axis=1))
    return jnp.concatenate(lines, axis=0).astype(jnp.bfloat16)


def row_sums(weights):
    return jnp.sum(weights.astype(jnp.float32), axis=1, keepdims=True)


def mine_body(runs, emb_width, kept_ref, mine_ref, part_ref, sums_ref):
    mine = mine_ref[:, :emb_width]
    weights = kernel_part(mine, mine, True, runs, kept_ref)
    part_ref[...] = weights
    sums_ref[...] = jnp.broadcast_to(row_sums(weights), sums_ref.shape)


def spread_body(
    emb_width, order, ranks, runs, rank_ref, kept_ref, part_ref, sums_ref, mine_ref, theirs_ref, out_ref, *scratch
):
    kernel_ref, root_ref, label_ref = scratch
    chips = len(order)
    team = len(ranks)
    half = mine_ref.shape[0]
    piece = half // chips
    share = out_ref.shape[1]
    units = (mine_ref[:, :emb_width], theirs_ref[:, :emb_width])
    kernel_ref[:half, :half] = part_ref[...]
    degrees = [sums_ref[...], jnp.zeros((half, 1), jnp.float32)]
    across = kernel_part(units[0], units[1], False, runs, kept_ref)
    theirs = kernel_part(units[1], units[1], True, runs, kept_ref)
    back = across.T
    kernel_ref[:half, half:] = across
    kernel_ref[half:, :half] = back
    kernel_ref[half:, half:] = theirs
    degrees[0] = degrees[0] + row_sums(across)
    degrees[1] = jnp.broadcast_to(
        jnp.sum(back.astype(jnp.float32) + theirs.astype(jnp.float32), axis=1, keepdims=True),
        (half, share),
    )
    inv_root = lax.rsqrt(jnp.concatenate(degrees, axis=0))
    root_ref[...] = inv_root
    labels = jnp.concatenate([mine_ref[:, emb_width:], theirs_ref[:, emb_width:]], axis=0).astype(
        jnp.float32
    )
    label_ref[...] = (1.0 - MIXING) * labels
    scaled = (inv_root * labels).astype(jnp.bfloat16)
    shares = jnp.concatenate([inv_root * inv_root] * (2 * half // share), axis=1)
    passed = (shares * kernel_ref[...].astype(jnp.float32)).astype(jnp.bfloat16)
    chip, core = rank_ref[0] // CORES, rank_ref[0] % CORES
    gather_side = core ^ gather_flip(chip, chips)
    team_side = core ^ team_flip(chip, chips)
    own = []
    for rank in ranks:
        target = chip // team * team + rank
        side = team_side ^ team_flip(target, chips) ^ gather_flip(target, chips)
        place = jnp.where(target == order[0], 0, target + 1 * (target < order[0]))
        row = place * piece + half * (side ^ gather_side)
        own.append(pl.ds(pl.multiple_of(row, 16), piece))
    first = MIXING * jnp.concatenate([kernel_ref[rows, :] for rows in own], axis=0).astype(
        jnp.float32
    )
    own_labels = jnp.concatenate([label_ref[rows, :] for rows in own], axis=0)
    own_root = jnp.concatenate([root_ref[rows, :] for rows in own], axis=0)
    steps = first
    for iteration in range(ITERS - 1):
        steps = MIXING * jnp.dot(
            steps.astype(jnp.bfloat16), passed, preferred_element_type=jnp.float32
        ) + (1.0 - MIXING) * first
    spread = jnp.dot(steps.astype(jnp.bfloat16), scaled, preferred_element_type=jnp.float32)
    out_ref[...] = (own_root * spread + own_labels).astype(jnp.bfloat16)


def place_body(ranks, pieces_ref, out_ref):
    share = pieces_ref.shape[2]
    for place, rank in enumerate(ranks):
        out_ref[:, rank * share : (rank + 1) * share] = pieces_ref[place]


def whole_shards(embeddings, labels, tile_mask):
    piece_rows, emb_width = embeddings.shape
    channels = labels.shape[1]
    team = channels // SHARE
    devices = lax.axis_size(AXES)
    chips = devices // CORES
    half = chips * piece_rows
    width = emb_width + SHARE
    order = chip_order(chips)
    ranks = team_order(team)
    runs = block_runs(order, piece_rows)
    gathered = [
        [chip * CORES + (side ^ gather_flip(chip, chips)) for chip in order]
        for side in range(CORES)
    ]
    teams = [
        [chip * CORES + (side ^ team_flip(chip, chips)) for chip in (first + rank for rank in ranks)]
        for first in range(0, chips, team)
        for side in range(CORES)
    ]
    vmem = pl.BlockSpec(memory_space=pltpu.VMEM)
    hbm = pl.BlockSpec(memory_space=pltpu.HBM)
    smem = pl.BlockSpec(memory_space=pltpu.SMEM)
    room = pltpu.CompilerParams(vmem_limit_bytes=ROOM)
    sent, kept = pl.pallas_call(
        functools.partial(pack_body, order),
        out_shape=(
            jax.ShapeDtypeStruct((chips, piece_rows, width), jnp.bfloat16),
            jax.ShapeDtypeStruct(tile_mask.shape, jnp.int32),
        ),
        in_specs=[hbm, hbm, hbm],
        out_specs=(vmem, vmem),
        scratch_shapes=[
            pltpu.VMEM(embeddings.shape, embeddings.dtype),
            pltpu.VMEM(labels.shape, labels.dtype),
            pltpu.SemaphoreType.DMA((3,)),
        ],
        compiler_params=room,
    )(*(pltpu.with_memory_space_constraint(x, pltpu.HBM) for x in (embeddings, labels, tile_mask)))
    mine = lax.all_to_all(
        sent, AXES, split_axis=0, concat_axis=0, axis_index_groups=gathered, tiled=True
    ).reshape(half, width)
    theirs = lax.ppermute(mine, AXES, [(i, i ^ 1) for i in range(devices)])
    part, sums = pl.pallas_call(
        functools.partial(mine_body, runs, emb_width),
        out_shape=(
            jax.ShapeDtypeStruct((half, half), jnp.bfloat16),
            jax.ShapeDtypeStruct((half, SHARE), jnp.float32),
        ),
        in_specs=[vmem, vmem],
        out_specs=(vmem, vmem),
        compiler_params=room,
        cost_estimate=pl.CostEstimate(
            flops=2 * half * half * emb_width,
            bytes_accessed=2 * half * (half + emb_width),
            transcendentals=half * half,
        ),
    )(kept, mine)
    rank = lax.axis_index(AXES).astype(jnp.int32).reshape(1)
    team_out = pl.pallas_call(
        functools.partial(spread_body, emb_width, order, ranks, runs),
        out_shape=jax.ShapeDtypeStruct((team * piece_rows, SHARE), jnp.bfloat16),
        in_specs=[smem, vmem, vmem, vmem, vmem, vmem],
        out_specs=vmem,
        scratch_shapes=[
            pltpu.VMEM((2 * half, 2 * half), jnp.bfloat16),
            pltpu.VMEM((2 * half, SHARE), jnp.float32),
            pltpu.VMEM((2 * half, SHARE), jnp.float32),
        ],
        compiler_params=room,
    )(rank, kept, part, sums, mine, theirs)
    pieces = lax.all_to_all(
        team_out.reshape(team, piece_rows, SHARE),
        AXES,
        split_axis=0,
        concat_axis=0,
        axis_index_groups=teams,
        tiled=True,
    )
    return pl.pallas_call(
        functools.partial(place_body, ranks),
        out_shape=jax.ShapeDtypeStruct((piece_rows, channels), jnp.bfloat16),
        in_specs=[vmem],
        out_specs=vmem,
        compiler_params=room,
    )(pieces)


def solution(mesh):
    placed = (P(AXES, None), P(AXES, None), P())
    devices = mesh.devices.size

    def spread_labels(embeddings, labels, tile_mask):
        images = embeddings.shape[0]
        channels = labels.shape[1]
        whole = (
            images * images * 2 <= WHOLE_KERNEL_BYTES
            and images % (devices * 16) == 0
            and BLOCK % (images // devices * CORES) == 0
            and channels % SHARE == 0
            and devices % (channels // SHARE * CORES) == 0
        )
        return jax.shard_map(
            whole_shards if whole else shards,
            mesh=mesh,
            in_specs=placed,
            out_specs=P(AXES, None),
            check_vma=False,
        )(embeddings, labels, tile_mask)

    return spread_labels
```

```python
import functools
import math

import jax
import jax.numpy as jnp
from jax import lax
from jax.experimental import pallas as pl
from jax.experimental.pallas import tpu as pltpu
from jax.sharding import PartitionSpec as P

BLOCK = 256
ITERS = 2


MIXING = 0.9
SHARPNESS = 3.0
EPSILON = 1e-06


def unit_rows(embeddings):
    values = embeddings.astype(jnp.float32)
    return (values * lax.rsqrt(jnp.sum(values * values, axis=1, keepdims=True) + EPSILON)).astype(
        jnp.bfloat16
    )


def symmetric_keep(tile_mask):
    blocks = tile_mask.shape[0]
    block_row = lax.broadcasted_iota(jnp.int32, (blocks, blocks), 0)
    block_col = lax.broadcasted_iota(jnp.int32, (blocks, blocks), 1)
    mirrored = jnp.where(block_row < block_col, tile_mask, tile_mask.T)
    return (jnp.where(block_row == block_col, 1, mirrored), block_row, block_col)


def rotate_rows(values, start):
    total = values.shape[0]
    doubled = jnp.concatenate([values, values], axis=0)
    return lax.dynamic_slice_in_dim(doubled, start, total, 0)


def one_term(operands):
    row_kernel, part_labels = operands
    return jnp.dot(row_kernel, part_labels, preferred_element_type=jnp.float32)


def no_term(operands):
    row_kernel, part_labels = operands
    return jnp.zeros((row_kernel.shape[0], part_labels.shape[1]), jnp.float32)


def shards(embeddings, labels, tile_mask):
    row_count = lax.axis_size("row")
    col_count = lax.axis_size("col")
    row_index = lax.axis_index("row")
    col_index = lax.axis_index("col")
    piece_rows = embeddings.shape[0]
    emb_width = embeddings.shape[1]
    channels = labels.shape[1]
    blocks = tile_mask.shape[0]
    sharpness = SHARPNESS * math.sqrt(emb_width)
    unit_vecs = unit_rows(embeddings)
    row_units = lax.all_gather(unit_vecs, "col", axis=0, tiled=True)
    col_gathered = lax.all_gather(unit_vecs, "row", axis=0, tiled=True)
    row_total = row_units.shape[0]
    col_total = col_gathered.shape[0]
    shift = row_index * piece_rows
    col_units = rotate_rows(col_gathered, shift)
    unit_count = math.gcd(8, row_count)
    unit_width = col_total // unit_count
    kept_sym, block_row, block_col = symmetric_keep(tile_mask)
    global_rows = row_index * row_total + jnp.arange(row_total, dtype=jnp.int32)
    row_blocks = global_rows // BLOCK
    block_ids = jnp.arange(blocks, dtype=jnp.int32)
    row_onehot = (row_blocks[:, None] == block_ids[None, :]).astype(jnp.bfloat16)
    row_table = jnp.dot(
        row_onehot, kept_sym.astype(jnp.bfloat16), preferred_element_type=jnp.float32
    ).astype(jnp.bfloat16)
    local_cols = (jnp.arange(col_total, dtype=jnp.int32) + shift) % col_total
    global_cols = (
        local_cols // piece_rows * col_count + col_index
    ) * piece_rows + local_cols % piece_rows
    col_blocks = global_cols // BLOCK
    kernels_row = []
    active_flags = []
    row_degree = jnp.zeros((row_total,), jnp.float32)
    for column_unit in range(unit_count):
        offset_cols = column_unit * unit_width
        part_units = col_units[offset_cols : offset_cols + unit_width]
        part_blocks = col_blocks[offset_cols : offset_cols + unit_width]
        part_cols = global_cols[offset_cols : offset_cols + unit_width]
        col_onehot = (part_blocks[:, None] == block_ids[None, :]).astype(jnp.bfloat16)
        kept_mask = lax.dot_general(
            row_table, col_onehot, (((1,), (1,)), ((), ())), preferred_element_type=jnp.float32
        )
        cosine = lax.dot_general(
            row_units, part_units, (((1,), (1,)), ((), ())), preferred_element_type=jnp.float32
        )
        distinct = global_rows[:, None] != part_cols[None, :]
        weights = jnp.where(
            distinct, jnp.exp(sharpness * cosine) * kept_mask, jnp.zeros_like(cosine)
        ).astype(jnp.bfloat16)
        active_flags.append(jnp.sum(kept_mask) > 0.0)
        kernels_row.append(weights)
        row_degree = row_degree + jnp.sum(weights, axis=1, dtype=jnp.float32)
    degree = lax.psum_scatter(row_degree, "col", scatter_dimension=0, tiled=True)
    inv_root = lax.rsqrt(degree)
    seed_scores = labels.astype(jnp.float32)
    current = seed_scores
    for iteration in range(ITERS):
        scaled = (inv_root[:, None] * current).astype(jnp.bfloat16)
        col_labels = rotate_rows(lax.all_gather(scaled, "row", axis=0, tiled=True), shift)
        row_sum = jnp.zeros((row_total, channels), jnp.float32)
        for column_unit in range(unit_count):
            offset_cols = column_unit * unit_width
            part_labels = col_labels[offset_cols : offset_cols + unit_width]
            row_sum = row_sum + lax.cond(
                active_flags[column_unit],
                one_term,
                no_term,
                (kernels_row[column_unit], part_labels),
            )
        sent_rows = row_sum.astype(jnp.bfloat16).reshape(col_count, piece_rows, channels)
        arrived = lax.all_to_all(sent_rows, "col", split_axis=0, concat_axis=0, tiled=True)
        spread = jnp.sum(arrived, axis=0, dtype=jnp.float32)
        current = MIXING * inv_root[:, None] * spread + (1.0 - MIXING) * seed_scores
    return current.astype(jnp.bfloat16)


AXES = ("row", "col")
CORES = 2
SHARE = 128
WHOLE_KERNEL_BYTES = 4 * 1024 * 1024
ROOM = 8 * 1024 * 1024


def chip_order(chips):
    first = chips // 2 + chips // 4 - 1
    return [first] + [chip for chip in range(chips) if chip != first]


def team_order(team):
    return [team - 1] + list(range(team - 1))


def gather_flip(chip, chips):
    return 1 * (chip >= chips // 2)


def team_flip(chip, chips):
    return 1 * (chip > 0) * (chip < chips // 2)


def pack_body(order, emb_hbm, lab_hbm, mask_hbm, sent_ref, kept_ref, emb_ref, lab_ref, sems):
    copies = [
        pltpu.make_async_copy(source, target, sems.at[k])
        for k, (source, target) in enumerate(
            ((emb_hbm, emb_ref), (lab_hbm, lab_ref), (mask_hbm, kept_ref))
        )
    ]
    for copy in copies:
        copy.start()
    peers, _, width = sent_ref.shape
    emb_width = emb_ref.shape[1]
    share = width - emb_width
    team = lab_ref.shape[1] // share
    copies[0].wait()
    unit_vecs = unit_rows(emb_ref[...])
    for peer in range(peers):
        sent_ref[peer, :, :emb_width] = unit_vecs
    copies[1].wait()
    for peer in range(peers):
        first = order[peer] % team * share
        sent_ref[peer, :, emb_width:] = lab_ref[:, first : first + share]
    copies[2].wait()


def block_runs(order, piece):
    runs = []
    for place, chip in enumerate(order):
        block = chip * CORES * piece // BLOCK
        if runs and runs[-1][2] == block:
            runs[-1][1] += piece
        else:
            runs.append([place * piece, (place + 1) * piece, block])
    return runs


def kernel_part(left, right, same, runs, kept_ref):
    sharpness = SHARPNESS * math.sqrt(left.shape[1])
    cosine = lax.dot_general(
        left, right, (((1,), (1,)), ((), ())), preferred_element_type=jnp.float32
    )
    weights = jnp.exp(sharpness * cosine)
    if same:
        row_ids = lax.broadcasted_iota(jnp.int32, weights.shape, 0)
        col_ids = lax.broadcasted_iota(jnp.int32, weights.shape, 1)
        weights = jnp.where(row_ids == col_ids, 0.0, weights)
    lines = []
    for row, row_end, i in runs:
        line = []
        for col, col_end, j in runs:
            part = weights[row:row_end, col:col_end]
            if i != j:
                low, high = min(i, j), max(i, j)
                part = part * kept_ref[low : low + 1, high : high + 1].astype(jnp.float32)
            line.append(part)
        lines.append(jnp.concatenate(line, axis=1))
    return jnp.concatenate(lines, axis=0).astype(jnp.bfloat16)


def row_sums(weights):
    return jnp.sum(weights.astype(jnp.float32), axis=1, keepdims=True)


def mine_body(runs, emb_width, kept_ref, mine_ref, part_ref, sums_ref):
    mine = mine_ref[:, :emb_width]
    weights = kernel_part(mine, mine, True, runs, kept_ref)
    part_ref[...] = weights
    sums_ref[...] = jnp.broadcast_to(row_sums(weights), sums_ref.shape)


def spread_body(
    emb_width, order, ranks, runs, rank_ref, kept_ref, part_ref, sums_ref, mine_ref, theirs_ref, out_ref, *scratch
):
    kernel_ref, root_ref, label_ref = scratch
    chips = len(order)
    team = len(ranks)
    half = mine_ref.shape[0]
    piece = half // chips
    share = out_ref.shape[1]
    units = (mine_ref[:, :emb_width], theirs_ref[:, :emb_width])
    kernel_ref[:half, :half] = part_ref[...]
    degrees = [sums_ref[...], jnp.zeros((half, 1), jnp.float32)]
    across = kernel_part(units[0], units[1], False, runs, kept_ref)
    theirs = kernel_part(units[1], units[1], True, runs, kept_ref)
    back = across.T
    kernel_ref[:half, half:] = across
    kernel_ref[half:, :half] = back
    kernel_ref[half:, half:] = theirs
    degrees[0] = degrees[0] + row_sums(across)
    degrees[1] = jnp.broadcast_to(
        jnp.sum(back.astype(jnp.float32) + theirs.astype(jnp.float32), axis=1, keepdims=True),
        (half, share),
    )
    labels = jnp.concatenate([mine_ref[:, emb_width:], theirs_ref[:, emb_width:]], axis=0).astype(
        jnp.float32
    )
    weights = kernel_ref[...]
    inv_root = lax.rsqrt(jnp.concatenate(degrees, axis=0))
    root_ref[...] = MIXING * inv_root
    kept_part = (1.0 - MIXING) * labels
    label_ref[...] = kept_part
    current = labels
    for iteration in range(ITERS - 1):
        scaled = (inv_root * current).astype(jnp.bfloat16)
        spread = jnp.dot(weights, scaled, preferred_element_type=jnp.float32)
        current = MIXING * inv_root * spread + kept_part
    scaled = (inv_root * current).astype(jnp.bfloat16)
    chip, core = rank_ref[0] // CORES, rank_ref[0] % CORES
    gather_side = core ^ gather_flip(chip, chips)
    team_side = core ^ team_flip(chip, chips)
    own = []
    for rank in ranks:
        target = chip // team * team + rank
        side = team_side ^ team_flip(target, chips) ^ gather_flip(target, chips)
        place = jnp.where(target == order[0], 0, target + 1 * (target < order[0]))
        row = place * piece + half * (side ^ gather_side)
        own.append(pl.ds(pl.multiple_of(row, 16), piece))
    own_weights = jnp.concatenate([kernel_ref[rows, :] for rows in own], axis=0)
    own_labels = jnp.concatenate([label_ref[rows, :] for rows in own], axis=0)
    own_root = jnp.concatenate([root_ref[rows, :] for rows in own], axis=0)
    spread = jnp.dot(own_weights, scaled, preferred_element_type=jnp.float32)
    out_ref[...] = (own_root * spread + own_labels).astype(jnp.bfloat16)


def place_body(ranks, pieces_ref, out_ref):
    share = pieces_ref.shape[2]
    for place, rank in enumerate(ranks):
        out_ref[:, rank * share : (rank + 1) * share] = pieces_ref[place]


def whole_shards(embeddings, labels, tile_mask):
    piece_rows, emb_width = embeddings.shape
    channels = labels.shape[1]
    team = channels // SHARE
    devices = lax.axis_size(AXES)
    chips = devices // CORES
    half = chips * piece_rows
    width = emb_width + SHARE
    order = chip_order(chips)
    ranks = team_order(team)
    runs = block_runs(order, piece_rows)
    gathered = [
        [chip * CORES + (side ^ gather_flip(chip, chips)) for chip in order]
        for side in range(CORES)
    ]
    teams = [
        [chip * CORES + (side ^ team_flip(chip, chips)) for chip in (first + rank for rank in ranks)]
        for first in range(0, chips, team)
        for side in range(CORES)
    ]
    vmem = pl.BlockSpec(memory_space=pltpu.VMEM)
    hbm = pl.BlockSpec(memory_space=pltpu.HBM)
    smem = pl.BlockSpec(memory_space=pltpu.SMEM)
    room = pltpu.CompilerParams(vmem_limit_bytes=ROOM)
    sent, kept = pl.pallas_call(
        functools.partial(pack_body, order),
        out_shape=(
            jax.ShapeDtypeStruct((chips, piece_rows, width), jnp.bfloat16),
            jax.ShapeDtypeStruct(tile_mask.shape, jnp.int32),
        ),
        in_specs=[hbm, hbm, hbm],
        out_specs=(vmem, vmem),
        scratch_shapes=[
            pltpu.VMEM(embeddings.shape, embeddings.dtype),
            pltpu.VMEM(labels.shape, labels.dtype),
            pltpu.SemaphoreType.DMA((3,)),
        ],
        compiler_params=room,
    )(*(pltpu.with_memory_space_constraint(x, pltpu.HBM) for x in (embeddings, labels, tile_mask)))
    mine = lax.all_to_all(
        sent, AXES, split_axis=0, concat_axis=0, axis_index_groups=gathered, tiled=True
    ).reshape(half, width)
    theirs = lax.ppermute(mine, AXES, [(i, i ^ 1) for i in range(devices)])
    part, sums = pl.pallas_call(
        functools.partial(mine_body, runs, emb_width),
        out_shape=(
            jax.ShapeDtypeStruct((half, half), jnp.bfloat16),
            jax.ShapeDtypeStruct((half, SHARE), jnp.float32),
        ),
        in_specs=[vmem, vmem],
        out_specs=(vmem, vmem),
        compiler_params=room,
        cost_estimate=pl.CostEstimate(
            flops=2 * half * half * emb_width,
            bytes_accessed=2 * half * (half + emb_width),
            transcendentals=half * half,
        ),
    )(kept, mine)
    rank = lax.axis_index(AXES).astype(jnp.int32).reshape(1)
    team_out = pl.pallas_call(
        functools.partial(spread_body, emb_width, order, ranks, runs),
        out_shape=jax.ShapeDtypeStruct((team * piece_rows, SHARE), jnp.bfloat16),
        in_specs=[smem, vmem, vmem, vmem, vmem, vmem],
        out_specs=vmem,
        scratch_shapes=[
            pltpu.VMEM((2 * half, 2 * half), jnp.bfloat16),
            pltpu.VMEM((2 * half, SHARE), jnp.float32),
            pltpu.VMEM((2 * half, SHARE), jnp.float32),
        ],
        compiler_params=room,
    )(rank, kept, part, sums, mine, theirs)
    pieces = lax.all_to_all(
        team_out.reshape(team, piece_rows, SHARE),
        AXES,
        split_axis=0,
        concat_axis=0,
        axis_index_groups=teams,
        tiled=True,
    )
    return pl.pallas_call(
        functools.partial(place_body, ranks),
        out_shape=jax.ShapeDtypeStruct((piece_rows, channels), jnp.bfloat16),
        in_specs=[vmem],
        out_specs=vmem,
        compiler_params=room,
    )(pieces)


def solution(mesh):
    placed = (P(AXES, None), P(AXES, None), P())
    devices = mesh.devices.size

    def spread_labels(embeddings, labels, tile_mask):
        images = embeddings.shape[0]
        channels = labels.shape[1]
        whole = (
            images * images * 2 <= WHOLE_KERNEL_BYTES
            and images % (devices * 16) == 0
            and BLOCK % (images // devices * CORES) == 0
            and channels % SHARE == 0
            and devices % (channels // SHARE * CORES) == 0
        )
        return jax.shard_map(
            whole_shards if whole else shards,
            mesh=mesh,
            in_specs=placed,
            out_specs=P(AXES, None),
            check_vma=False,
        )(embeddings, labels, tile_mask)

    return spread_labels
```

```python
import functools
import math

import jax
import jax.numpy as jnp
from jax import lax
from jax.experimental import pallas as pl
from jax.experimental.pallas import tpu as pltpu
from jax.sharding import PartitionSpec as P

BLOCK = 256
ITERS = 2


MIXING = 0.9
SHARPNESS = 3.0
EPSILON = 1e-06


def unit_rows(embeddings):
    values = embeddings.astype(jnp.float32)
    return (values * lax.rsqrt(jnp.sum(values * values, axis=1, keepdims=True) + EPSILON)).astype(
        jnp.bfloat16
    )


def symmetric_keep(tile_mask):
    blocks = tile_mask.shape[0]
    block_row = lax.broadcasted_iota(jnp.int32, (blocks, blocks), 0)
    block_col = lax.broadcasted_iota(jnp.int32, (blocks, blocks), 1)
    mirrored = jnp.where(block_row < block_col, tile_mask, tile_mask.T)
    return (jnp.where(block_row == block_col, 1, mirrored), block_row, block_col)


def rotate_rows(values, start):
    total = values.shape[0]
    doubled = jnp.concatenate([values, values], axis=0)
    return lax.dynamic_slice_in_dim(doubled, start, total, 0)


def one_term(operands):
    row_kernel, part_labels = operands
    return jnp.dot(row_kernel, part_labels, preferred_element_type=jnp.float32)


def no_term(operands):
    row_kernel, part_labels = operands
    return jnp.zeros((row_kernel.shape[0], part_labels.shape[1]), jnp.float32)


def shards(embeddings, labels, tile_mask):
    row_count = lax.axis_size("row")
    col_count = lax.axis_size("col")
    row_index = lax.axis_index("row")
    col_index = lax.axis_index("col")
    piece_rows = embeddings.shape[0]
    emb_width = embeddings.shape[1]
    channels = labels.shape[1]
    blocks = tile_mask.shape[0]
    sharpness = SHARPNESS * math.sqrt(emb_width)
    unit_vecs = unit_rows(embeddings)
    row_units = lax.all_gather(unit_vecs, "col", axis=0, tiled=True)
    col_gathered = lax.all_gather(unit_vecs, "row", axis=0, tiled=True)
    row_total = row_units.shape[0]
    col_total = col_gathered.shape[0]
    shift = row_index * piece_rows
    col_units = rotate_rows(col_gathered, shift)
    unit_count = math.gcd(8, row_count)
    unit_width = col_total // unit_count
    kept_sym, block_row, block_col = symmetric_keep(tile_mask)
    global_rows = row_index * row_total + jnp.arange(row_total, dtype=jnp.int32)
    row_blocks = global_rows // BLOCK
    block_ids = jnp.arange(blocks, dtype=jnp.int32)
    row_onehot = (row_blocks[:, None] == block_ids[None, :]).astype(jnp.bfloat16)
    row_table = jnp.dot(
        row_onehot, kept_sym.astype(jnp.bfloat16), preferred_element_type=jnp.float32
    ).astype(jnp.bfloat16)
    local_cols = (jnp.arange(col_total, dtype=jnp.int32) + shift) % col_total
    global_cols = (
        local_cols // piece_rows * col_count + col_index
    ) * piece_rows + local_cols % piece_rows
    col_blocks = global_cols // BLOCK
    kernels_row = []
    active_flags = []
    row_degree = jnp.zeros((row_total,), jnp.float32)
    for column_unit in range(unit_count):
        offset_cols = column_unit * unit_width
        part_units = col_units[offset_cols : offset_cols + unit_width]
        part_blocks = col_blocks[offset_cols : offset_cols + unit_width]
        part_cols = global_cols[offset_cols : offset_cols + unit_width]
        col_onehot = (part_blocks[:, None] == block_ids[None, :]).astype(jnp.bfloat16)
        kept_mask = lax.dot_general(
            row_table, col_onehot, (((1,), (1,)), ((), ())), preferred_element_type=jnp.float32
        )
        cosine = lax.dot_general(
            row_units, part_units, (((1,), (1,)), ((), ())), preferred_element_type=jnp.float32
        )
        distinct = global_rows[:, None] != part_cols[None, :]
        weights = jnp.where(
            distinct, jnp.exp(sharpness * cosine) * kept_mask, jnp.zeros_like(cosine)
        ).astype(jnp.bfloat16)
        active_flags.append(jnp.sum(kept_mask) > 0.0)
        kernels_row.append(weights)
        row_degree = row_degree + jnp.sum(weights, axis=1, dtype=jnp.float32)
    degree = lax.psum_scatter(row_degree, "col", scatter_dimension=0, tiled=True)
    inv_root = lax.rsqrt(degree)
    seed_scores = labels.astype(jnp.float32)
    current = seed_scores
    for iteration in range(ITERS):
        scaled = (inv_root[:, None] * current).astype(jnp.bfloat16)
        col_labels = rotate_rows(lax.all_gather(scaled, "row", axis=0, tiled=True), shift)
        row_sum = jnp.zeros((row_total, channels), jnp.float32)
        for column_unit in range(unit_count):
            offset_cols = column_unit * unit_width
            part_labels = col_labels[offset_cols : offset_cols + unit_width]
            row_sum = row_sum + lax.cond(
                active_flags[column_unit],
                one_term,
                no_term,
                (kernels_row[column_unit], part_labels),
            )
        sent_rows = row_sum.astype(jnp.bfloat16).reshape(col_count, piece_rows, channels)
        arrived = lax.all_to_all(sent_rows, "col", split_axis=0, concat_axis=0, tiled=True)
        spread = jnp.sum(arrived, axis=0, dtype=jnp.float32)
        current = MIXING * inv_root[:, None] * spread + (1.0 - MIXING) * seed_scores
    return current.astype(jnp.bfloat16)


AXES = ("row", "col")
CORES = 2
SHARE = 128
WHOLE_KERNEL_BYTES = 4 * 1024 * 1024
ROOM = 8 * 1024 * 1024


def chip_order(chips):
    first = chips // 2 + chips // 4 - 1
    return [first] + [chip for chip in range(chips) if chip != first]


def team_order(team):
    planes = [rank for pair in zip(range(team // 2), range(team // 2, team)) for rank in pair]
    return [team - 1] + planes[:-1]


def gather_flip(chip, chips):
    return 1 * (chip >= chips // 2)


def team_flip(chip, chips):
    return 1 * (chip > 0) * (chip < chips // 2)


def pack_body(order, emb_hbm, lab_hbm, mask_hbm, sent_ref, kept_ref, emb_ref, lab_ref, sems):
    copies = [
        pltpu.make_async_copy(source, target, sems.at[k])
        for k, (source, target) in enumerate(
            ((emb_hbm, emb_ref), (lab_hbm, lab_ref), (mask_hbm, kept_ref))
        )
    ]
    for copy in copies:
        copy.start()
    peers, _, width = sent_ref.shape
    emb_width = emb_ref.shape[1]
    share = width - emb_width
    team = lab_ref.shape[1] // share
    copies[0].wait()
    unit_vecs = unit_rows(emb_ref[...])
    for peer in range(peers):
        sent_ref[peer, :, :emb_width] = unit_vecs
    copies[1].wait()
    for peer in range(peers):
        first = order[peer] % team * share
        sent_ref[peer, :, emb_width:] = lab_ref[:, first : first + share]
    copies[2].wait()


def block_runs(order, piece):
    runs = []
    for place, chip in enumerate(order):
        block = chip * CORES * piece // BLOCK
        if runs and runs[-1][2] == block:
            runs[-1][1] += piece
        else:
            runs.append([place * piece, (place + 1) * piece, block])
    return runs


def kernel_part(left, right, same, runs, kept_ref):
    sharpness = SHARPNESS * math.sqrt(left.shape[1])
    cosine = lax.dot_general(
        left, right, (((1,), (1,)), ((), ())), preferred_element_type=jnp.float32
    )
    weights = jnp.exp(sharpness * cosine)
    if same:
        row_ids = lax.broadcasted_iota(jnp.int32, weights.shape, 0)
        col_ids = lax.broadcasted_iota(jnp.int32, weights.shape, 1)
        weights = jnp.where(row_ids == col_ids, 0.0, weights)
    lines = []
    for row, row_end, i in runs:
        line = []
        for col, col_end, j in runs:
            part = weights[row:row_end, col:col_end]
            if i != j:
                low, high = min(i, j), max(i, j)
                part = part * kept_ref[low : low + 1, high : high + 1].astype(jnp.float32)
            line.append(part)
        lines.append(jnp.concatenate(line, axis=1))
    return jnp.concatenate(lines, axis=0).astype(jnp.bfloat16)


def row_sums(weights):
    return jnp.sum(weights.astype(jnp.float32), axis=1, keepdims=True)


def mine_body(runs, emb_width, kept_ref, mine_ref, part_ref, sums_ref):
    mine = mine_ref[:, :emb_width]
    weights = kernel_part(mine, mine, True, runs, kept_ref)
    part_ref[...] = weights
    sums_ref[...] = jnp.broadcast_to(row_sums(weights), sums_ref.shape)


def spread_body(
    emb_width, order, ranks, runs, rank_ref, kept_ref, part_ref, sums_ref, mine_ref, theirs_ref, out_ref, *scratch
):
    kernel_ref, root_ref, label_ref = scratch
    chips = len(order)
    team = len(ranks)
    half = mine_ref.shape[0]
    piece = half // chips
    share = out_ref.shape[1]
    units = (mine_ref[:, :emb_width], theirs_ref[:, :emb_width])
    kernel_ref[:half, :half] = part_ref[...]
    degrees = [sums_ref[...], jnp.zeros((half, 1), jnp.float32)]
    across = kernel_part(units[0], units[1], False, runs, kept_ref)
    theirs = kernel_part(units[1], units[1], True, runs, kept_ref)
    back = across.T
    kernel_ref[:half, half:] = across
    kernel_ref[half:, :half] = back
    kernel_ref[half:, half:] = theirs
    degrees[0] = degrees[0] + row_sums(across)
    degrees[1] = jnp.broadcast_to(
        jnp.sum(back.astype(jnp.float32) + theirs.astype(jnp.float32), axis=1, keepdims=True),
        (half, share),
    )
    labels = jnp.concatenate([mine_ref[:, emb_width:], theirs_ref[:, emb_width:]], axis=0).astype(
        jnp.float32
    )
    weights = kernel_ref[...]
    inv_root = lax.rsqrt(jnp.concatenate(degrees, axis=0))
    root_ref[...] = MIXING * inv_root
    kept_part = (1.0 - MIXING) * labels
    label_ref[...] = kept_part
    current = labels
    for iteration in range(ITERS - 1):
        scaled = (inv_root * current).astype(jnp.bfloat16)
        spread = jnp.dot(weights, scaled, preferred_element_type=jnp.float32)
        current = MIXING * inv_root * spread + kept_part
    scaled = (inv_root * current).astype(jnp.bfloat16)
    chip, core = rank_ref[0] // CORES, rank_ref[0] % CORES
    gather_side = core ^ gather_flip(chip, chips)
    team_side = core ^ team_flip(chip, chips)
    own = []
    for rank in ranks:
        target = chip // team * team + rank
        side = team_side ^ team_flip(target, chips) ^ gather_flip(target, chips)
        place = jnp.where(target == order[0], 0, target + 1 * (target < order[0]))
        row = place * piece + half * (side ^ gather_side)
        own.append(pl.ds(pl.multiple_of(row, 16), piece))
    own_weights = jnp.concatenate([kernel_ref[rows, :] for rows in own], axis=0)
    own_labels = jnp.concatenate([label_ref[rows, :] for rows in own], axis=0)
    own_root = jnp.concatenate([root_ref[rows, :] for rows in own], axis=0)
    spread = jnp.dot(own_weights, scaled, preferred_element_type=jnp.float32)
    out_ref[...] = (own_root * spread + own_labels).astype(jnp.bfloat16)


def place_body(ranks, pieces_ref, out_ref):
    share = pieces_ref.shape[2]
    for place, rank in enumerate(ranks):
        out_ref[:, rank * share : (rank + 1) * share] = pieces_ref[place]


def whole_shards(embeddings, labels, tile_mask):
    piece_rows, emb_width = embeddings.shape
    channels = labels.shape[1]
    team = channels // SHARE
    devices = lax.axis_size(AXES)
    chips = devices // CORES
    half = chips * piece_rows
    width = emb_width + SHARE
    order = chip_order(chips)
    ranks = team_order(team)
    runs = block_runs(order, piece_rows)
    gathered = [
        [chip * CORES + (side ^ gather_flip(chip, chips)) for chip in order]
        for side in range(CORES)
    ]
    teams = [
        [chip * CORES + (side ^ team_flip(chip, chips)) for chip in (first + rank for rank in ranks)]
        for first in range(0, chips, team)
        for side in range(CORES)
    ]
    vmem = pl.BlockSpec(memory_space=pltpu.VMEM)
    hbm = pl.BlockSpec(memory_space=pltpu.HBM)
    smem = pl.BlockSpec(memory_space=pltpu.SMEM)
    room = pltpu.CompilerParams(vmem_limit_bytes=ROOM)
    sent, kept = pl.pallas_call(
        functools.partial(pack_body, order),
        out_shape=(
            jax.ShapeDtypeStruct((chips, piece_rows, width), jnp.bfloat16),
            jax.ShapeDtypeStruct(tile_mask.shape, jnp.int32),
        ),
        in_specs=[hbm, hbm, hbm],
        out_specs=(vmem, vmem),
        scratch_shapes=[
            pltpu.VMEM(embeddings.shape, embeddings.dtype),
            pltpu.VMEM(labels.shape, labels.dtype),
            pltpu.SemaphoreType.DMA((3,)),
        ],
        compiler_params=room,
    )(*(pltpu.with_memory_space_constraint(x, pltpu.HBM) for x in (embeddings, labels, tile_mask)))
    mine = lax.all_to_all(
        sent, AXES, split_axis=0, concat_axis=0, axis_index_groups=gathered, tiled=True
    ).reshape(half, width)
    theirs = lax.ppermute(mine, AXES, [(i, i ^ 1) for i in range(devices)])
    part, sums = pl.pallas_call(
        functools.partial(mine_body, runs, emb_width),
        out_shape=(
            jax.ShapeDtypeStruct((half, half), jnp.bfloat16),
            jax.ShapeDtypeStruct((half, SHARE), jnp.float32),
        ),
        in_specs=[vmem, vmem],
        out_specs=(vmem, vmem),
        compiler_params=room,
        cost_estimate=pl.CostEstimate(
            flops=2 * half * half * emb_width,
            bytes_accessed=2 * half * (half + emb_width),
            transcendentals=half * half,
        ),
    )(kept, mine)
    rank = lax.axis_index(AXES).astype(jnp.int32).reshape(1)
    team_out = pl.pallas_call(
        functools.partial(spread_body, emb_width, order, ranks, runs),
        out_shape=jax.ShapeDtypeStruct((team * piece_rows, SHARE), jnp.bfloat16),
        in_specs=[smem, vmem, vmem, vmem, vmem, vmem],
        out_specs=vmem,
        scratch_shapes=[
            pltpu.VMEM((2 * half, 2 * half), jnp.bfloat16),
            pltpu.VMEM((2 * half, SHARE), jnp.float32),
            pltpu.VMEM((2 * half, SHARE), jnp.float32),
        ],
        compiler_params=room,
    )(rank, kept, part, sums, mine, theirs)
    pieces = lax.all_to_all(
        team_out.reshape(team, piece_rows, SHARE),
        AXES,
        split_axis=0,
        concat_axis=0,
        axis_index_groups=teams,
        tiled=True,
    )
    return pl.pallas_call(
        functools.partial(place_body, ranks),
        out_shape=jax.ShapeDtypeStruct((piece_rows, channels), jnp.bfloat16),
        in_specs=[vmem],
        out_specs=vmem,
        compiler_params=room,
    )(pieces)


def solution(mesh):
    placed = (P(AXES, None), P(AXES, None), P())
    devices = mesh.devices.size

    def spread_labels(embeddings, labels, tile_mask):
        images = embeddings.shape[0]
        channels = labels.shape[1]
        whole = (
            images * images * 2 <= WHOLE_KERNEL_BYTES
            and images % (devices * 16) == 0
            and BLOCK % (images // devices * CORES) == 0
            and channels % SHARE == 0
            and devices % (channels // SHARE * CORES) == 0
        )
        return jax.shard_map(
            whole_shards if whole else shards,
            mesh=mesh,
            in_specs=placed,
            out_specs=P(AXES, None),
            check_vma=False,
        )(embeddings, labels, tile_mask)

    return spread_labels
```

```python
import functools
import math

import jax
import jax.numpy as jnp
from jax import lax
from jax.experimental import pallas as pl
from jax.experimental.pallas import tpu as pltpu
from jax.sharding import PartitionSpec as P

BLOCK = 256
ITERS = 2


MIXING = 0.9
SHARPNESS = 3.0
EPSILON = 1e-06


def unit_rows(embeddings):
    values = embeddings.astype(jnp.float32)
    return (values * lax.rsqrt(jnp.sum(values * values, axis=1, keepdims=True) + EPSILON)).astype(
        jnp.bfloat16
    )


def symmetric_keep(tile_mask):
    blocks = tile_mask.shape[0]
    block_row = lax.broadcasted_iota(jnp.int32, (blocks, blocks), 0)
    block_col = lax.broadcasted_iota(jnp.int32, (blocks, blocks), 1)
    mirrored = jnp.where(block_row < block_col, tile_mask, tile_mask.T)
    return (jnp.where(block_row == block_col, 1, mirrored), block_row, block_col)


def rotate_rows(values, start):
    total = values.shape[0]
    doubled = jnp.concatenate([values, values], axis=0)
    return lax.dynamic_slice_in_dim(doubled, start, total, 0)


def one_term(operands):
    row_kernel, part_labels = operands
    return jnp.dot(row_kernel, part_labels, preferred_element_type=jnp.float32)


def no_term(operands):
    row_kernel, part_labels = operands
    return jnp.zeros((row_kernel.shape[0], part_labels.shape[1]), jnp.float32)


def shards(embeddings, labels, tile_mask):
    row_count = lax.axis_size("row")
    col_count = lax.axis_size("col")
    row_index = lax.axis_index("row")
    col_index = lax.axis_index("col")
    piece_rows = embeddings.shape[0]
    emb_width = embeddings.shape[1]
    channels = labels.shape[1]
    blocks = tile_mask.shape[0]
    sharpness = SHARPNESS * math.sqrt(emb_width)
    unit_vecs = unit_rows(embeddings)
    row_units = lax.all_gather(unit_vecs, "col", axis=0, tiled=True)
    col_gathered = lax.all_gather(unit_vecs, "row", axis=0, tiled=True)
    row_total = row_units.shape[0]
    col_total = col_gathered.shape[0]
    shift = row_index * piece_rows
    col_units = rotate_rows(col_gathered, shift)
    unit_count = math.gcd(8, row_count)
    unit_width = col_total // unit_count
    kept_sym, block_row, block_col = symmetric_keep(tile_mask)
    global_rows = row_index * row_total + jnp.arange(row_total, dtype=jnp.int32)
    row_blocks = global_rows // BLOCK
    block_ids = jnp.arange(blocks, dtype=jnp.int32)
    row_onehot = (row_blocks[:, None] == block_ids[None, :]).astype(jnp.bfloat16)
    row_table = jnp.dot(
        row_onehot, kept_sym.astype(jnp.bfloat16), preferred_element_type=jnp.float32
    ).astype(jnp.bfloat16)
    local_cols = (jnp.arange(col_total, dtype=jnp.int32) + shift) % col_total
    global_cols = (
        local_cols // piece_rows * col_count + col_index
    ) * piece_rows + local_cols % piece_rows
    col_blocks = global_cols // BLOCK
    kernels_row = []
    active_flags = []
    row_degree = jnp.zeros((row_total,), jnp.float32)
    for column_unit in range(unit_count):
        offset_cols = column_unit * unit_width
        part_units = col_units[offset_cols : offset_cols + unit_width]
        part_blocks = col_blocks[offset_cols : offset_cols + unit_width]
        part_cols = global_cols[offset_cols : offset_cols + unit_width]
        col_onehot = (part_blocks[:, None] == block_ids[None, :]).astype(jnp.bfloat16)
        kept_mask = lax.dot_general(
            row_table, col_onehot, (((1,), (1,)), ((), ())), preferred_element_type=jnp.float32
        )
        cosine = lax.dot_general(
            row_units, part_units, (((1,), (1,)), ((), ())), preferred_element_type=jnp.float32
        )
        distinct = global_rows[:, None] != part_cols[None, :]
        weights = jnp.where(
            distinct, jnp.exp(sharpness * cosine) * kept_mask, jnp.zeros_like(cosine)
        ).astype(jnp.bfloat16)
        active_flags.append(jnp.sum(kept_mask) > 0.0)
        kernels_row.append(weights)
        row_degree = row_degree + jnp.sum(weights, axis=1, dtype=jnp.float32)
    degree = lax.psum_scatter(row_degree, "col", scatter_dimension=0, tiled=True)
    inv_root = lax.rsqrt(degree)
    seed_scores = labels.astype(jnp.float32)
    current = seed_scores
    for iteration in range(ITERS):
        scaled = (inv_root[:, None] * current).astype(jnp.bfloat16)
        col_labels = rotate_rows(lax.all_gather(scaled, "row", axis=0, tiled=True), shift)
        row_sum = jnp.zeros((row_total, channels), jnp.float32)
        for column_unit in range(unit_count):
            offset_cols = column_unit * unit_width
            part_labels = col_labels[offset_cols : offset_cols + unit_width]
            row_sum = row_sum + lax.cond(
                active_flags[column_unit],
                one_term,
                no_term,
                (kernels_row[column_unit], part_labels),
            )
        sent_rows = row_sum.astype(jnp.bfloat16).reshape(col_count, piece_rows, channels)
        arrived = lax.all_to_all(sent_rows, "col", split_axis=0, concat_axis=0, tiled=True)
        spread = jnp.sum(arrived, axis=0, dtype=jnp.float32)
        current = MIXING * inv_root[:, None] * spread + (1.0 - MIXING) * seed_scores
    return current.astype(jnp.bfloat16)


AXES = ("row", "col")
CORES = 2
SHARE = 128
WHOLE_KERNEL_BYTES = 4 * 1024 * 1024
ROOM = 8 * 1024 * 1024


def chip_order(chips):
    first = chips // 2 + chips // 4 - 1
    return [first] + [chip for chip in range(chips) if chip != first]


def team_order(team):
    return [team - 1] + list(range(team - 1))


def gather_flip(chip, chips):
    return 1 * (chip >= chips // 2)


def team_flip(chip, chips):
    return 1 * (chip > 0) * (chip < chips // 2)


def pack_body(order, emb_hbm, lab_hbm, mask_hbm, sent_ref, kept_ref, emb_ref, lab_ref, sems):
    copies = [
        pltpu.make_async_copy(source, target, sems.at[k])
        for k, (source, target) in enumerate(
            ((emb_hbm, emb_ref), (lab_hbm, lab_ref), (mask_hbm, kept_ref))
        )
    ]
    for copy in copies:
        copy.start()
    peers, _, width = sent_ref.shape
    emb_width = emb_ref.shape[1]
    share = width - emb_width
    team = lab_ref.shape[1] // share
    copies[0].wait()
    unit_vecs = unit_rows(emb_ref[...])
    for peer in range(peers):
        sent_ref[peer, :, :emb_width] = unit_vecs
    copies[1].wait()
    for peer in range(peers):
        first = order[peer] % team * share
        sent_ref[peer, :, emb_width:] = lab_ref[:, first : first + share]
    copies[2].wait()


def block_runs(order, piece):
    runs = []
    for place, chip in enumerate(order):
        block = chip * CORES * piece // BLOCK
        if runs and runs[-1][2] == block:
            runs[-1][1] += piece
        else:
            runs.append([place * piece, (place + 1) * piece, block])
    return runs


def kernel_part(left, right, same, runs, kept_ref):
    sharpness = SHARPNESS * math.sqrt(left.shape[1])
    cosine = lax.dot_general(
        left, right, (((1,), (1,)), ((), ())), preferred_element_type=jnp.float32
    )
    weights = jnp.exp(sharpness * cosine)
    if same:
        row_ids = lax.broadcasted_iota(jnp.int32, weights.shape, 0)
        col_ids = lax.broadcasted_iota(jnp.int32, weights.shape, 1)
        weights = jnp.where(row_ids == col_ids, 0.0, weights)
    lines = []
    for row, row_end, i in runs:
        line = []
        for col, col_end, j in runs:
            part = weights[row:row_end, col:col_end]
            if i != j:
                low, high = min(i, j), max(i, j)
                part = part * kept_ref[low : low + 1, high : high + 1].astype(jnp.float32)
            line.append(part)
        lines.append(jnp.concatenate(line, axis=1))
    return jnp.concatenate(lines, axis=0).astype(jnp.bfloat16)


def row_sums(weights):
    return jnp.sum(weights.astype(jnp.float32), axis=1, keepdims=True)


def mine_body(runs, emb_width, kept_ref, mine_ref, part_ref, sums_ref):
    mine = mine_ref[:, :emb_width]
    weights = kernel_part(mine, mine, True, runs, kept_ref)
    part_ref[...] = weights
    sums_ref[...] = jnp.broadcast_to(row_sums(weights), sums_ref.shape)


def spread_body(
    emb_width, order, ranks, runs, rank_ref, kept_ref, part_ref, sums_ref, mine_ref, theirs_ref, out_ref, *scratch
):
    kernel_ref, root_ref, label_ref = scratch
    chips = len(order)
    team = len(ranks)
    half = mine_ref.shape[0]
    piece = half // chips
    share = out_ref.shape[1]
    units = (mine_ref[:, :emb_width], theirs_ref[:, :emb_width])
    kernel_ref[:half, :half] = part_ref[...]
    degrees = [sums_ref[...], jnp.zeros((half, 1), jnp.float32)]
    across = kernel_part(units[0], units[1], False, runs, kept_ref)
    theirs = kernel_part(units[1], units[1], True, runs, kept_ref)
    back = across.T
    kernel_ref[:half, half:] = across
    kernel_ref[half:, :half] = back
    kernel_ref[half:, half:] = theirs
    degrees[0] = degrees[0] + row_sums(across)
    degrees[1] = jnp.broadcast_to(
        jnp.sum(back.astype(jnp.float32) + theirs.astype(jnp.float32), axis=1, keepdims=True),
        (half, share),
    )
    inv_root = lax.rsqrt(jnp.concatenate(degrees, axis=0))
    root_ref[...] = inv_root
    labels = jnp.concatenate([mine_ref[:, emb_width:], theirs_ref[:, emb_width:]], axis=0).astype(
        jnp.float32
    )
    label_ref[...] = (1.0 - MIXING) * labels
    scaled = (inv_root * labels).astype(jnp.bfloat16)
    shares = [inv_root[side * half : (side + 1) * half] for side in range(2)]
    shares = [jnp.concatenate([part * part] * (half // share), axis=1) for part in shares]
    passed = jnp.concatenate(
        [
            jnp.concatenate(
                [(shares[row] * part.astype(jnp.float32)).astype(jnp.bfloat16) for part in line], axis=1
            )
            for row, line in enumerate(((part_ref[...], across), (back, theirs)))
        ],
        axis=0,
    )
    chip, core = rank_ref[0] // CORES, rank_ref[0] % CORES
    gather_side = core ^ gather_flip(chip, chips)
    team_side = core ^ team_flip(chip, chips)
    own = []
    for rank in ranks:
        target = chip // team * team + rank
        side = team_side ^ team_flip(target, chips) ^ gather_flip(target, chips)
        place = jnp.where(target == order[0], 0, target + 1 * (target < order[0]))
        row = place * piece + half * (side ^ gather_side)
        own.append(pl.ds(pl.multiple_of(row, 16), piece))
    first = MIXING * jnp.concatenate([kernel_ref[rows, :] for rows in own], axis=0).astype(
        jnp.float32
    )
    own_labels = jnp.concatenate([label_ref[rows, :] for rows in own], axis=0)
    own_root = jnp.concatenate([root_ref[rows, :] for rows in own], axis=0)
    steps = first
    for iteration in range(ITERS - 1):
        steps = MIXING * jnp.dot(
            steps.astype(jnp.bfloat16), passed, preferred_element_type=jnp.float32
        ) + (1.0 - MIXING) * first
    spread = jnp.dot(steps.astype(jnp.bfloat16), scaled, preferred_element_type=jnp.float32)
    out_ref[...] = (own_root * spread + own_labels).astype(jnp.bfloat16)


def place_body(ranks, pieces_ref, out_ref):
    share = pieces_ref.shape[2]
    for place, rank in enumerate(ranks):
        out_ref[:, rank * share : (rank + 1) * share] = pieces_ref[place]


def whole_shards(embeddings, labels, tile_mask):
    piece_rows, emb_width = embeddings.shape
    channels = labels.shape[1]
    team = channels // SHARE
    devices = lax.axis_size(AXES)
    chips = devices // CORES
    half = chips * piece_rows
    width = emb_width + SHARE
    order = chip_order(chips)
    ranks = team_order(team)
    runs = block_runs(order, piece_rows)
    gathered = [
        [chip * CORES + (side ^ gather_flip(chip, chips)) for chip in order]
        for side in range(CORES)
    ]
    teams = [
        [chip * CORES + (side ^ team_flip(chip, chips)) for chip in (first + rank for rank in ranks)]
        for first in range(0, chips, team)
        for side in range(CORES)
    ]
    vmem = pl.BlockSpec(memory_space=pltpu.VMEM)
    hbm = pl.BlockSpec(memory_space=pltpu.HBM)
    smem = pl.BlockSpec(memory_space=pltpu.SMEM)
    room = pltpu.CompilerParams(vmem_limit_bytes=ROOM)
    sent, kept = pl.pallas_call(
        functools.partial(pack_body, order),
        out_shape=(
            jax.ShapeDtypeStruct((chips, piece_rows, width), jnp.bfloat16),
            jax.ShapeDtypeStruct(tile_mask.shape, jnp.int32),
        ),
        in_specs=[hbm, hbm, hbm],
        out_specs=(vmem, vmem),
        scratch_shapes=[
            pltpu.VMEM(embeddings.shape, embeddings.dtype),
            pltpu.VMEM(labels.shape, labels.dtype),
            pltpu.SemaphoreType.DMA((3,)),
        ],
        compiler_params=room,
    )(*(pltpu.with_memory_space_constraint(x, pltpu.HBM) for x in (embeddings, labels, tile_mask)))
    mine = lax.all_to_all(
        sent, AXES, split_axis=0, concat_axis=0, axis_index_groups=gathered, tiled=True
    ).reshape(half, width)
    theirs = lax.ppermute(mine, AXES, [(i, i ^ 1) for i in range(devices)])
    part, sums = pl.pallas_call(
        functools.partial(mine_body, runs, emb_width),
        out_shape=(
            jax.ShapeDtypeStruct((half, half), jnp.bfloat16),
            jax.ShapeDtypeStruct((half, SHARE), jnp.float32),
        ),
        in_specs=[vmem, vmem],
        out_specs=(vmem, vmem),
        compiler_params=room,
        cost_estimate=pl.CostEstimate(
            flops=2 * half * half * emb_width,
            bytes_accessed=2 * half * (half + emb_width),
            transcendentals=half * half,
        ),
    )(kept, mine)
    rank = lax.axis_index(AXES).astype(jnp.int32).reshape(1)
    team_out = pl.pallas_call(
        functools.partial(spread_body, emb_width, order, ranks, runs),
        out_shape=jax.ShapeDtypeStruct((team * piece_rows, SHARE), jnp.bfloat16),
        in_specs=[smem, vmem, vmem, vmem, vmem, vmem],
        out_specs=vmem,
        scratch_shapes=[
            pltpu.VMEM((2 * half, 2 * half), jnp.bfloat16),
            pltpu.VMEM((2 * half, SHARE), jnp.float32),
            pltpu.VMEM((2 * half, SHARE), jnp.float32),
        ],
        compiler_params=room,
    )(rank, kept, part, sums, mine, theirs)
    pieces = lax.all_to_all(
        team_out.reshape(team, piece_rows, SHARE),
        AXES,
        split_axis=0,
        concat_axis=0,
        axis_index_groups=teams,
        tiled=True,
    )
    return pl.pallas_call(
        functools.partial(place_body, ranks),
        out_shape=jax.ShapeDtypeStruct((piece_rows, channels), jnp.bfloat16),
        in_specs=[vmem],
        out_specs=vmem,
        compiler_params=room,
    )(pieces)


def solution(mesh):
    placed = (P(AXES, None), P(AXES, None), P())
    devices = mesh.devices.size

    def spread_labels(embeddings, labels, tile_mask):
        images = embeddings.shape[0]
        channels = labels.shape[1]
        whole = (
            images * images * 2 <= WHOLE_KERNEL_BYTES
            and images % (devices * 16) == 0
            and BLOCK % (images // devices * CORES) == 0
            and channels % SHARE == 0
            and devices % (channels // SHARE * CORES) == 0
        )
        return jax.shard_map(
            whole_shards if whole else shards,
            mesh=mesh,
            in_specs=placed,
            out_specs=P(AXES, None),
            check_vma=False,
        )(embeddings, labels, tile_mask)

    return spread_labels
```
